512 devices in a mesh: head: 8 (over x_hi, y), ctx: 64 (over z, x_lo, core).
Axes of the slice: x: 4 (x_hi: 2, x_lo: 2; x = x_hi * 2 + x_lo), y: 4, z: 16, core: 2. Of those that a mesh axis runs over, the one named last changes fastest.
Arguments:
- queries: bfloat16 [32768, 64, 128], P(('ctx', 'head')), may hold values from -6 to 6
- keys: bfloat16 [32768, 8, 128], P(('ctx', 'head')), may hold values from -6 to 6
- values: bfloat16 [32768, 8, 128], P(('ctx', 'head')), may hold values from -6 to 6
- out_grad: bfloat16 [32768, 64, 128], P(('ctx', 'head')), may hold values from -6 to 6
- doc_lengths: int32 [48], replicated, may hold values from 1 to 1024, 32768 in all
- stored_block_order: int32 [256], replicated, may hold values from 0 to 255, as said below
Outputs:
- attended: bfloat16 [32768, 64, 128], P(('ctx', 'head'))
- query_grad: bfloat16 [32768, 64, 128], P(('ctx', 'head'))
- key_gradient: bfloat16 [32768, 8, 128], P(('ctx', 'head'))
- value_gradient: bfloat16 [32768, 8, 128], P(('ctx', 'head'))
The draws below stay inside these ranges and needn't reach their ends.
Inputs may be any that keep to these rules, and one draw needn't show every extreme that they name: `doc_lengths`: they sum to 32768 and the largest is exactly 1024. A permutation in which stored_block_order[b] // 4 = b // 4: the stored blocks of each aligned group of 4 are that group's sequence blocks in some order.
All inputs are finite; a program needn't handle non-finite values.
Results may differ from the reference program's by a relative error of at most 0.039.
Values may be sent and summed in bfloat16 or wider, within the bound.
No kernel may reach another device: no remote copies, remote signals or barrier semaphores. Data moves between devices by JAX's collectives and lax.ppermute only.
A program may use at most 64 MiB of HBM per device.

```python
import math
import jax
import jax.numpy as jnp
import numpy as np
from jax import lax

QUERY_HEADS = 64
KEY_VALUE_HEADS = 8
HEAD_SIZE = 128
BLOCK_TOKENS = 128
BLK_DEV = 4
DOCS = 48
STORED_BLOCKS = 256
SEQUENCE_TOKENS = 32768
DOC_MOST = 1024


def shared_keys(key):
    key_offset_base = jax.random.fold_in(key, 0)
    unpermuted_keys = jnp.clip(jax.random.normal(key_offset_base, (SEQUENCE_TOKENS, KEY_VALUE_HEADS, HEAD_SIZE), jnp.float32), -5.5, 5.5)
    return unpermuted_keys


def draw_keys(key, part):
    unpermuted_keys = shared_keys(key)
    return unpermuted_keys.astype(jnp.bfloat16)


def draw_queries(key, part):
    key = jax.random.fold_in(key, 5)
    drawn_rows = jnp.clip(jax.random.normal(key, (SEQUENCE_TOKENS, QUERY_HEADS, HEAD_SIZE), jnp.float32), -5.5, 5.5)
    return drawn_rows.astype(jnp.bfloat16)


def draw_stored_block_order(key, part):
    key = jax.random.fold_in(key, 7)
    groups = STORED_BLOCKS // BLK_DEV
    group_keys = jax.random.split(key, groups)
    shuffled = jax.vmap(lambda one_key: jax.random.permutation(one_key, BLK_DEV))(group_keys).astype(jnp.int32)
    starts = jnp.arange(groups, dtype=jnp.int32)[:, None] * BLK_DEV
    return (starts + shuffled).reshape(STORED_BLOCKS).astype(jnp.int32)


def steps_of(own_key, dims, pieces, low, high):
    def one(position, blocks):
        draws = jax.random.uniform(jax.random.fold_in(jax.random.fold_in(own_key, 6), position), (blocks,), jnp.float32, low / len(pieces), high / len(pieces))
        return jnp.repeat(jnp.exp(draws), dims[position] // blocks).reshape((-1,) + (1,) * (len(dims) - position - 1))

    level = one(*pieces[0])
    for cut in pieces[1:]:
        level = level * one(*cut)
    return level


def profile(count, total, reach, skew):
    portions = [(1 << 20) // math.isqrt(rank ** skew) + 1 for rank in range(2, count + 1)]
    rest, given = total - reach - (count - 1), [1] * (count - 1)
    while rest > 0:
        candidates = [i for i in range(count - 1) if given[i] < reach]
        whole, left = sum([portions[i] for i in candidates]), rest
        for i in candidates:
            more = min(reach - given[i], max(1, left * portions[i] // whole), rest)
            given[i] = given[i] + more
            rest = rest - more
    return np.array([reach] + given)


def ragged_sizes(own_key, number_of, total, reach, skew):
    if number_of == 2:
        one = jax.random.randint(own_key, (), max(1, total - reach), min(reach, total - 1) + 1)
        return jnp.stack([one, total - one])
    tallies = jnp.asarray(profile(number_of, total, reach, skew), jnp.int32)
    twos = (number_of - 1) // 2
    giver, sink = tallies[1:1 + 2 * twos:2], tallies[2:2 + 2 * twos:2]
    margin = jnp.minimum(giver - 1, reach - sink)
    passed = jax.random.randint(jax.random.fold_in(own_key, 1), (twos,), 0, 1 << 20) % (margin + 1)
    tallies = tallies.at[1:1 + 2 * twos:2].set(giver - passed).at[2:2 + 2 * twos:2].set(sink + passed)
    return tallies[jax.random.permutation(jax.random.fold_in(own_key, 2), number_of)]


def bell_draw(key, shape, scale, most, pieces=(), kind=jnp.bfloat16):
    array = jax.random.normal(key, shape, jnp.float32) * scale
    if len(pieces) > 0:
        array = steps_of(key, shape, pieces, -0.22, 0.18) * array
    return jnp.clip(array, min=-most, max=most).astype(kind)


def setup_inputs(seed: int = 0) -> dict:
    splits = jax.random.split(jax.random.key(seed), 7)
    queries = draw_queries(jax.random.fold_in(splits[6], 71), 0)
    keys = draw_keys(jax.random.fold_in(splits[6], 71), 0)
    values = bell_draw(splits[2], (SEQUENCE_TOKENS, KEY_VALUE_HEADS, HEAD_SIZE), 1.0, 6.0, ((0, 512),))
    out_grad = bell_draw(splits[3], (SEQUENCE_TOKENS, QUERY_HEADS, HEAD_SIZE), 1.0, 6.0, ((0, 512),))
    doc_lengths = ragged_sizes(splits[4], DOCS, SEQUENCE_TOKENS, DOC_MOST, 2).astype(jnp.int32)
    stored_block_order = draw_stored_block_order(jax.random.fold_in(splits[6], 71), 0)
    return dict(queries=queries, keys=keys, values=values, out_grad=out_grad, doc_lengths=doc_lengths, stored_block_order=stored_block_order)


neg_big = -1.0e30


def segment_ids(positions, doc_lengths):
    ends = jnp.cumsum(doc_lengths).astype(jnp.int32)
    return jnp.sum((positions[..., None] >= ends).astype(jnp.int32), axis=-1).astype(jnp.int32)


def lowered(values_in):
    return lax.optimization_barrier(values_in.astype(jnp.bfloat16)).astype(jnp.float32)


def reference(queries, keys, values, out_grad, doc_lengths, stored_block_order):
    score_scale = HEAD_SIZE ** -0.5
    sharing_count = QUERY_HEADS // KEY_VALUE_HEADS
    window_blocks = DOC_MOST // BLOCK_TOKENS + 1
    window_rows = window_blocks * BLOCK_TOKENS
    inverse = jnp.zeros((STORED_BLOCKS,), jnp.int32).at[stored_block_order].set(jnp.arange(STORED_BLOCKS, dtype=jnp.int32))

    def in_order(blocked_array):
        shaped = blocked_array.reshape((STORED_BLOCKS, BLOCK_TOKENS) + blocked_array.shape[1:])
        return shaped[inverse].reshape(blocked_array.shape)

    query_sequence = in_order(queries)
    key_seq = in_order(keys)
    value_seq = in_order(values)
    gradient_sequence = in_order(out_grad)
    doc_ids = segment_ids(jnp.arange(SEQUENCE_TOKENS, dtype=jnp.int32), doc_lengths)

    def block_step(running, block_index):
        key_accumulator, value_accumulator = running
        row_offset_start = (block_index * BLOCK_TOKENS).astype(jnp.int32)
        key_start = (jnp.clip(block_index + 1 - window_blocks, 0, STORED_BLOCKS - window_blocks) * BLOCK_TOKENS).astype(jnp.int32)
        query_block_rows = lax.dynamic_slice_in_dim(query_sequence, row_offset_start, BLOCK_TOKENS, 0).astype(jnp.float32).reshape(BLOCK_TOKENS, KEY_VALUE_HEADS, sharing_count, HEAD_SIZE)
        gradient_block = lax.dynamic_slice_in_dim(gradient_sequence, row_offset_start, BLOCK_TOKENS, 0).astype(jnp.float32).reshape(BLOCK_TOKENS, KEY_VALUE_HEADS, sharing_count, HEAD_SIZE)
        key_window = lax.dynamic_slice_in_dim(key_seq, key_start, window_rows, 0).astype(jnp.float32)
        value_window = lax.dynamic_slice_in_dim(value_seq, key_start, window_rows, 0).astype(jnp.float32)
        query_pos = row_offset_start + jnp.arange(BLOCK_TOKENS, dtype=jnp.int32)
        key_pos = key_start + jnp.arange(window_rows, dtype=jnp.int32)
        query_doc = lax.dynamic_slice_in_dim(doc_ids, row_offset_start, BLOCK_TOKENS, 0)
        key_doc = lax.dynamic_slice_in_dim(doc_ids, key_start, window_rows, 0)
        allowed = (query_doc[:, None] == key_doc[None, :]) & (key_pos[None, :] <= query_pos[:, None])
        scores = jnp.einsum("qhgd,khd->hgqk", query_block_rows, key_window) * score_scale
        row_max = jnp.max(jnp.where(allowed, scores, neg_big), axis=-1)
        row_total = jnp.sum(jnp.where(allowed, jnp.exp(scores - row_max[..., None]), 0.0), axis=-1)
        log_total = row_max + jnp.log(row_total)
        weights = jnp.where(allowed, jnp.exp(scores - log_total[..., None]), 0.0)
        weights_low = lowered(weights)
        attended_block = jnp.einsum("hgqk,khd->qhgd", weights_low, value_window).astype(jnp.bfloat16)
        row_delta = jnp.sum(gradient_block * attended_block.astype(jnp.float32), axis=-1).transpose(1, 2, 0)
        grad_weights = jnp.einsum("qhgd,khd->hgqk", gradient_block, value_window)
        grad_scores = lowered(weights * (grad_weights - row_delta[..., None]))
        query_part = jnp.einsum("hgqk,khd->qhgd", grad_scores, key_window) * score_scale
        key_part = jnp.einsum("hgqk,qhgd->khd", grad_scores, query_block_rows) * score_scale
        value_part = jnp.einsum("hgqk,qhgd->khd", weights_low, gradient_block)
        key_accumulator = lax.dynamic_update_slice_in_dim(key_accumulator, lax.dynamic_slice_in_dim(key_accumulator, key_start, window_rows, 0) + key_part, key_start, 0)
        value_accumulator = lax.dynamic_update_slice_in_dim(value_accumulator, lax.dynamic_slice_in_dim(value_accumulator, key_start, window_rows, 0) + value_part, key_start, 0)
        outputs = (attended_block.reshape(BLOCK_TOKENS, QUERY_HEADS, HEAD_SIZE), query_part.reshape(BLOCK_TOKENS, QUERY_HEADS, HEAD_SIZE).astype(jnp.bfloat16))
        return (key_accumulator, value_accumulator), outputs

    initial_accumulator = (jnp.zeros((SEQUENCE_TOKENS, KEY_VALUE_HEADS, HEAD_SIZE), jnp.float32), jnp.zeros((SEQUENCE_TOKENS, KEY_VALUE_HEADS, HEAD_SIZE), jnp.float32))
    (key_accumulator, value_accumulator), (attended_pos, query_pos_grad) = lax.scan(block_step, initial_accumulator, jnp.arange(STORED_BLOCKS, dtype=jnp.int32))
    attended = attended_pos[stored_block_order].reshape(SEQUENCE_TOKENS, QUERY_HEADS, HEAD_SIZE)
    query_grad = query_pos_grad[stored_block_order].reshape(SEQUENCE_TOKENS, QUERY_HEADS, HEAD_SIZE)
    key_gradient = key_accumulator.reshape(STORED_BLOCKS, BLOCK_TOKENS, KEY_VALUE_HEADS, HEAD_SIZE)[stored_block_order].reshape(SEQUENCE_TOKENS, KEY_VALUE_HEADS, HEAD_SIZE).astype(jnp.bfloat16)
    value_gradient = value_accumulator.reshape(STORED_BLOCKS, BLOCK_TOKENS, KEY_VALUE_HEADS, HEAD_SIZE)[stored_block_order].reshape(SEQUENCE_TOKENS, KEY_VALUE_HEADS, HEAD_SIZE).astype(jnp.bfloat16)
    return attended, query_grad, key_gradient, value_gradient
```

```python
import functools
import math

import jax
import jax.numpy as jnp
from jax import lax
from jax.experimental import pallas as pl
from jax.experimental.pallas import tpu as pltpu
from jax.sharding import PartitionSpec as P

HEAD_SIZE = 128
BLOCK = 128
CELL_BLOCKS = 4
SLOTS = 3
WINDOW_BLOCKS = SLOTS * CELL_BLOCKS
WINDOW = WINDOW_BLOCKS * BLOCK
CHUNK = 2 * BLOCK
PADDED = WINDOW + BLOCK
REACH = 10 * BLOCK
SHARE = 8
ROWS = BLOCK * SHARE
TILE = 256

SCALE = HEAD_SIZE ** (-0.5)
EXP2_SCALE = SCALE * math.log2(math.e)
NEG_BIG = -1e30

NT = (((1,), (1,)), ((), ()))
NN = (((1,), (0,)), ((), ()))


def dot(a, b, dims=NN):
    return lax.dot_general(a, b, dims, preferred_element_type=jnp.float32)


def passed_along(block, axis, distance):
    devices = range(lax.axis_size(axis))
    route = [(i - distance, i) for i in devices if i - distance in devices]
    return lax.ppermute(block, axis, route)


def stored_rows(kv_ref, block, which):
    first = kv_ref[2 * block, pl.ds(64 * which, 64), :]
    second = kv_ref[2 * block + 1, pl.ds(64 * which, 64), :]
    return jnp.concatenate([first, second], axis=0)


def window_start(scal_ref, slot, block):
    index = (SLOTS - 1 - slot) * CELL_BLOCKS + block
    return pl.multiple_of(scal_ref[index] * BLOCK, BLOCK)


def allowed_tile(key_start, doc_start, query_pos):
    key_pos = key_start + lax.broadcasted_iota(jnp.int32, (CHUNK, TILE), 0)
    return (key_pos >= doc_start) & (key_pos <= query_pos)


def row_positions(first_block, tile):
    lane = lax.broadcasted_iota(jnp.int32, (1, TILE), 1) + tile * TILE
    return first_block * BLOCK + lax.shift_right_logical(lane, 3)


def forward_kernel(scal_ref, q_ref, doc_ref, kv0_ref, kv1_ref, kv2_ref, out_ref, out_t_ref, lse_ref, key_seq, value_t, scores, acc, top):
    step = pl.program_id(0)

    @pl.when(step == 0)
    def _():
        for slot, kv_ref in enumerate((kv0_ref, kv1_ref, kv2_ref)):
            for block in range(CELL_BLOCKS):
                start = window_start(scal_ref, slot, block)
                key_seq[pl.ds(start, BLOCK), :] = stored_rows(kv_ref, block, 0)
                value = stored_rows(kv_ref, block, 1).astype(jnp.float32)
                value_t[:, pl.ds(start, BLOCK)] = value.T.astype(jnp.bfloat16)
        key_seq[pl.ds(WINDOW, BLOCK), :] = jnp.zeros((BLOCK, HEAD_SIZE), jnp.bfloat16)
        value_t[:, pl.ds(WINDOW, BLOCK)] = jnp.zeros((HEAD_SIZE, BLOCK), jnp.bfloat16)

    first_block = scal_ref[WINDOW_BLOCKS + step]
    low_block = scal_ref[WINDOW_BLOCKS + CELL_BLOCKS + step]
    chunks = lax.shift_right_logical(first_block - low_block + 2, 1)
    top[...] = jnp.full_like(top, NEG_BIG)
    acc[...] = jnp.zeros_like(acc)

    def score_chunk(turn, _):
        key_start = pl.multiple_of((low_block + 2 * turn) * BLOCK, BLOCK)
        keys = key_seq[pl.ds(key_start, CHUNK), :]
        for tile in range(ROWS // TILE):
            cols = pl.ds(tile * TILE, TILE)
            queries = q_ref[tile // 2, pl.ds((tile % 2) * TILE, TILE), :]
            raw = dot(keys, queries, NT)
            allowed = allowed_tile(key_start, doc_ref[0, :, cols], row_positions(first_block, tile))
            raw = jnp.where(allowed, raw, NEG_BIG)
            scores[pl.ds(pl.multiple_of(turn * CHUNK, CHUNK), CHUNK), cols] = raw
            part = jnp.max(raw.reshape(CHUNK // 8, 8, TILE), axis=0)
            top[:, cols] = jnp.maximum(top[:, cols], part)
        return 0

    lax.fori_loop(0, chunks, score_chunk, 0)
    highest = jnp.max(top[...], axis=0, keepdims=True) * EXP2_SCALE
    top[...] = jnp.zeros_like(top)

    def value_chunk(turn, _):
        key_start = pl.multiple_of((low_block + 2 * turn) * BLOCK, BLOCK)
        values = value_t[:, pl.ds(key_start, CHUNK)]
        for tile in range(ROWS // TILE):
            cols = pl.ds(tile * TILE, TILE)
            raw = scores[pl.ds(pl.multiple_of(turn * CHUNK, CHUNK), CHUNK), cols]
            weights = jnp.exp2(raw * EXP2_SCALE - highest[:, tile * TILE : (tile + 1) * TILE])
            top[:, cols] += jnp.sum(weights.reshape(CHUNK // 8, 8, TILE), axis=0)
            acc[:, cols] += dot(values, weights.astype(jnp.bfloat16))
        return 0

    lax.fori_loop(0, chunks, value_chunk, 0)
    total = jnp.sum(top[...], axis=0, keepdims=True)
    lse_ref[0] = highest + jnp.log2(total)
    out_t = acc[...] * (1.0 / total)
    out_t_ref[0] = out_t.astype(jnp.bfloat16)
    out = out_t.T.astype(jnp.bfloat16)
    out_ref[0] = out[: ROWS // 2]
    out_ref[1] = out[ROWS // 2 :]


def backward_kernel(scal_ref, q_ref, grad_ref, out_t_ref, lse_ref, doc_ref, kv0_ref, kv1_ref, kv2_ref, dq_ref, dkv0_ref, dkv1_ref, dkv2_ref, key_seq, value_seq, key_t, dk_acc, dv_acc, dq_t, weights_low, grads_low, delta):
    step = pl.program_id(0)

    @pl.when(step == 0)
    def _():
        for slot, kv_ref in enumerate((kv0_ref, kv1_ref, kv2_ref)):
            for block in range(CELL_BLOCKS):
                start = window_start(scal_ref, slot, block)
                key = stored_rows(kv_ref, block, 0)
                key_seq[pl.ds(start, BLOCK), :] = key
                key_t[:, pl.ds(start, BLOCK)] = key.astype(jnp.float32).T.astype(jnp.bfloat16)
                value_seq[pl.ds(start, BLOCK), :] = stored_rows(kv_ref, block, 1)
        zeros = jnp.zeros((BLOCK, HEAD_SIZE), jnp.bfloat16)
        key_seq[pl.ds(WINDOW, BLOCK), :] = zeros
        value_seq[pl.ds(WINDOW, BLOCK), :] = zeros
        key_t[:, pl.ds(WINDOW, BLOCK)] = zeros
        dk_acc[...] = jnp.zeros_like(dk_acc)
        dv_acc[...] = jnp.zeros_like(dv_acc)

    first_block = scal_ref[WINDOW_BLOCKS + step]
    low_block = scal_ref[WINDOW_BLOCKS + CELL_BLOCKS + step]
    chunks = lax.shift_right_logical(first_block - low_block + 2, 1)
    dq_t[...] = jnp.zeros_like(dq_t)
    for half in range(2):
        cols = slice(half * ROWS // 2, (half + 1) * ROWS // 2)
        grad_t = grad_ref[half].astype(jnp.float32).T
        delta[:, cols] = jnp.sum(grad_t * out_t_ref[0, :, cols].astype(jnp.float32), axis=0, keepdims=True)

    def chunk(turn, _):
        key_start = pl.multiple_of((low_block + 2 * turn) * BLOCK, BLOCK)
        keys = key_seq[pl.ds(key_start, CHUNK), :]
        values = value_seq[pl.ds(key_start, CHUNK), :]
        for tile in range(ROWS // TILE):
            cols = pl.ds(tile * TILE, TILE)
            half, rows = tile // 2, pl.ds((tile % 2) * TILE, TILE)
            raw = dot(keys, q_ref[half, rows, :], NT)
            allowed = allowed_tile(key_start, doc_ref[0, :, cols], row_positions(first_block, tile))
            weights = jnp.exp2(jnp.where(allowed, raw * EXP2_SCALE - lse_ref[0, :, cols], NEG_BIG))
            weights_low[:, cols] = weights.astype(jnp.bfloat16)
            sent = dot(values, grad_ref[half, rows, :], NT)
            grads = (weights * (sent - delta[:, cols])).astype(jnp.bfloat16)
            grads_low[:, cols] = grads
            dq_t[:, cols] += dot(key_t[:, pl.ds(key_start, CHUNK)], grads)
        queries = jnp.concatenate([q_ref[0], q_ref[1]], axis=0)
        out_grads = jnp.concatenate([grad_ref[0], grad_ref[1]], axis=0)
        dk_acc[pl.ds(key_start, CHUNK), :] += dot(grads_low[...], queries)
        dv_acc[pl.ds(key_start, CHUNK), :] += dot(weights_low[...], out_grads)
        return 0

    lax.fori_loop(0, chunks, chunk, 0)
    query_grad = (dq_t[...] * SCALE).T.astype(jnp.bfloat16)
    dq_ref[0] = query_grad[: ROWS // 2]
    dq_ref[1] = query_grad[ROWS // 2 :]

    @pl.when(step == CELL_BLOCKS - 1)
    def _():
        for slot, dkv_ref in enumerate((dkv0_ref, dkv1_ref, dkv2_ref)):
            for block in range(CELL_BLOCKS):
                start = window_start(scal_ref, slot, block)
                dk = (dk_acc[pl.ds(start, BLOCK), :] * SCALE).astype(jnp.bfloat16)
                dv = dv_acc[pl.ds(start, BLOCK), :].astype(jnp.bfloat16)
                for half in range(2):
                    rows = slice(half * 64, (half + 1) * 64)
                    dkv_ref[2 * block + half, pl.ds(0, 64), :] = dk[rows]
                    dkv_ref[2 * block + half, pl.ds(64, 64), :] = dv[rows]


def row_spec():
    return pl.BlockSpec((2, ROWS // 2, HEAD_SIZE), lambda b, s: (b, 0, 0))


def lane_spec(rows):
    return pl.BlockSpec((1, rows, ROWS), lambda b, s: (b, 0, 0))


def kv_spec():
    return pl.BlockSpec((8, 128, HEAD_SIZE), lambda b, s: (0, 0, 0))


def params():
    return pltpu.CompilerParams(dimension_semantics=("arbitrary",), vmem_limit_bytes=40 * 1024 * 1024)


def forward(scal, q_in, doc_rows, kv):
    return pl.pallas_call(
        forward_kernel,
        grid_spec=pltpu.PrefetchScalarGridSpec(
            num_scalar_prefetch=1,
            grid=(CELL_BLOCKS,),
            in_specs=[row_spec(), lane_spec(1), kv_spec(), kv_spec(), kv_spec()],
            out_specs=[row_spec(), lane_spec(HEAD_SIZE), lane_spec(1)],
            scratch_shapes=[
                pltpu.VMEM((PADDED, HEAD_SIZE), jnp.bfloat16),
                pltpu.VMEM((HEAD_SIZE, PADDED), jnp.bfloat16),
                pltpu.VMEM((REACH, ROWS), jnp.float32),
                pltpu.VMEM((HEAD_SIZE, ROWS), jnp.float32),
                pltpu.VMEM((8, ROWS), jnp.float32),
            ],
        ),
        out_shape=[
            jax.ShapeDtypeStruct((8, ROWS // 2, HEAD_SIZE), jnp.bfloat16),
            jax.ShapeDtypeStruct((CELL_BLOCKS, HEAD_SIZE, ROWS), jnp.bfloat16),
            jax.ShapeDtypeStruct((CELL_BLOCKS, 1, ROWS), jnp.float32),
        ],
        compiler_params=params(),
        cost_estimate=pl.CostEstimate(flops=4_000_000_000, bytes_accessed=4_000_000, transcendentals=4_000_000),
        name="forward",
    )(scal, q_in, doc_rows, *kv)


def backward(scal, q_in, grad_in, out_t, lse, doc_rows, kv):
    dkv_shape = jax.ShapeDtypeStruct((8, 128, HEAD_SIZE), jnp.bfloat16)
    return pl.pallas_call(
        backward_kernel,
        grid_spec=pltpu.PrefetchScalarGridSpec(
            num_scalar_prefetch=1,
            grid=(CELL_BLOCKS,),
            in_specs=[row_spec(), row_spec(), lane_spec(HEAD_SIZE), lane_spec(1), lane_spec(1), kv_spec(), kv_spec(), kv_spec()],
            out_specs=[row_spec(), kv_spec(), kv_spec(), kv_spec()],
            scratch_shapes=[
                pltpu.VMEM((PADDED, HEAD_SIZE), jnp.bfloat16),
                pltpu.VMEM((PADDED, HEAD_SIZE), jnp.bfloat16),
                pltpu.VMEM((HEAD_SIZE, PADDED), jnp.bfloat16),
                pltpu.VMEM((PADDED, HEAD_SIZE), jnp.float32),
                pltpu.VMEM((PADDED, HEAD_SIZE), jnp.float32),
                pltpu.VMEM((HEAD_SIZE, ROWS), jnp.float32),
                pltpu.VMEM((CHUNK, ROWS), jnp.bfloat16),
                pltpu.VMEM((CHUNK, ROWS), jnp.bfloat16),
                pltpu.VMEM((1, ROWS), jnp.float32),
            ],
        ),
        out_shape=[jax.ShapeDtypeStruct((8, ROWS // 2, HEAD_SIZE), jnp.bfloat16), dkv_shape, dkv_shape, dkv_shape],
        compiler_params=params(),
        cost_estimate=pl.CostEstimate(flops=10_000_000_000, bytes_accessed=6_000_000, transcendentals=4_000_000),
        name="backward",
    )(scal, q_in, grad_in, out_t, lse, doc_rows, *kv)


def by_head(rows):
    tokens = rows.shape[0]
    split = rows.reshape(tokens, 8, -1, HEAD_SIZE).transpose(1, 0, 2, 3)
    return split.reshape(8, -1, HEAD_SIZE)


def exchanged(block):
    return lax.all_to_all(block, "head", split_axis=0, concat_axis=0, tiled=True)


def plan(doc_lengths, stored_block_order):
    cell = lax.axis_index("ctx")
    starts = jnp.cumsum(doc_lengths) - doc_lengths
    window_first = (cell - (SLOTS - 1)) * CELL_BLOCKS
    padded = jnp.pad(stored_block_order, (WINDOW_BLOCKS - CELL_BLOCKS, 0))
    window_order = lax.dynamic_slice_in_dim(padded, cell * CELL_BLOCKS, WINDOW_BLOCKS, 0)
    base = jnp.arange(WINDOW_BLOCKS, dtype=jnp.int32) // CELL_BLOCKS * CELL_BLOCKS
    place = base + window_order % CELL_BLOCKS
    own_place = place[WINDOW_BLOCKS - CELL_BLOCKS :]
    own_block = window_first + own_place
    token = lax.broadcasted_iota(jnp.int32, (CELL_BLOCKS, 1, ROWS), 2) // SHARE
    pos = own_block[:, None, None] * BLOCK + token
    begun = starts <= pos[..., None]
    doc_start = jnp.max(jnp.where(begun, starts, 0), axis=-1)
    doc_rows = doc_start - window_first * BLOCK
    low = jnp.max(jnp.where(starts <= own_block[:, None] * BLOCK, starts, 0), axis=-1)
    low_block = low // BLOCK - window_first
    scal = jnp.concatenate([place, own_place, low_block]).astype(jnp.int32)
    return scal, doc_rows.astype(jnp.int32)


def body(queries, keys, values, out_grad, doc_lengths, stored_block_order):
    scal, doc_rows = plan(doc_lengths, stored_block_order)
    first_in = exchanged(jnp.concatenate([by_head(queries), by_head(keys), by_head(values)], axis=1))
    kv0 = first_in[:, 512:, :]
    kv1 = passed_along(kv0, "ctx", 1)
    kv2 = passed_along(kv1, "ctx", 1)
    grad_in = exchanged(by_head(out_grad))
    kv = (kv0, kv1, kv2)
    attended_loc, out_t, lse = forward(scal, first_in, doc_rows, kv)
    attended_in = exchanged(attended_loc)
    query_grad_loc, dkv0, dkv1, dkv2 = backward(scal, first_in, grad_in, out_t, lse, doc_rows, kv)
    carried = passed_along(dkv2, "ctx", -1).astype(jnp.float32) + dkv1.astype(jnp.float32)
    carried = passed_along(carried.astype(jnp.bfloat16), "ctx", -1).astype(jnp.float32) + dkv0.astype(jnp.float32)
    last_in = exchanged(jnp.concatenate([query_grad_loc, carried.astype(jnp.bfloat16)], axis=1))
    tokens = queries.shape[0]

    def by_token(block, heads):
        return block.reshape(8, tokens, heads, HEAD_SIZE).transpose(1, 0, 2, 3).reshape(tokens, -1, HEAD_SIZE)

    attended = by_token(attended_in, SHARE)
    query_grad = by_token(last_in[:, :512], SHARE)
    key_gradient = by_token(last_in[:, 512:576], 1)
    value_gradient = by_token(last_in[:, 576:], 1)
    return attended, query_grad, key_gradient, value_gradient


def solution(mesh):
    spec = P(("ctx", "head"), None, None)
    return jax.shard_map(
        body,
        mesh=mesh,
        in_specs=(spec, spec, spec, spec, P(), P()),
        out_specs=(spec, spec, spec, spec),
        check_vma=False,
    )
```

```python
import functools
import math

import jax
import jax.numpy as jnp
from jax import lax
from jax.experimental import pallas as pl
from jax.experimental.pallas import tpu as pltpu
from jax.sharding import PartitionSpec as P

HEAD_SIZE = 128
BLOCK = 128
CELL_BLOCKS = 4
SLOTS = 3
WINDOW_BLOCKS = SLOTS * CELL_BLOCKS
WINDOW = WINDOW_BLOCKS * BLOCK
CHUNK = 2 * BLOCK
PADDED = WINDOW + BLOCK
REACH = 10 * BLOCK
SHARE = 8
ROWS = BLOCK * SHARE
TILE = 256

SCALE = HEAD_SIZE ** (-0.5)
EXP2_SCALE = SCALE * math.log2(math.e)
NEG_BIG = -1e30

NT = (((1,), (1,)), ((), ()))
NN = (((1,), (0,)), ((), ()))


def dot(a, b, dims=NN):
    return lax.dot_general(a, b, dims, preferred_element_type=jnp.float32)


def passed_along(block, axis, distance):
    devices = range(lax.axis_size(axis))
    route = [(i - distance, i) for i in devices if i - distance in devices]
    return lax.ppermute(block, axis, route)


def stored_rows(kv_ref, block, which):
    first = kv_ref[2 * block, pl.ds(64 * which, 64), :]
    second = kv_ref[2 * block + 1, pl.ds(64 * which, 64), :]
    return jnp.concatenate([first, second], axis=0)


def window_start(scal_ref, slot, block):
    index = (SLOTS - 1 - slot) * CELL_BLOCKS + block
    return pl.multiple_of(scal_ref[index] * BLOCK, BLOCK)


def allowed_tile(key_start, doc_start, query_pos):
    key_pos = key_start + lax.broadcasted_iota(jnp.int32, (CHUNK, TILE), 0)
    return (key_pos >= doc_start) & (key_pos <= query_pos)


def row_positions(first_block, tile):
    lane = lax.broadcasted_iota(jnp.int32, (1, TILE), 1) + tile * TILE
    return first_block * BLOCK + lax.shift_right_logical(lane, 3)


def forward_kernel(scal_ref, q_ref, doc_ref, kv0_ref, kv1_ref, kv2_ref, out_ref, out_t_ref, lse_ref, key_seq, value_t, scores, acc, top):
    step = pl.program_id(0)

    @pl.when(step == 0)
    def _():
        for slot, kv_ref in enumerate((kv0_ref, kv1_ref, kv2_ref)):
            for block in range(CELL_BLOCKS):
                start = window_start(scal_ref, slot, block)
                key_seq[pl.ds(start, BLOCK), :] = stored_rows(kv_ref, block, 0)
                value = stored_rows(kv_ref, block, 1).astype(jnp.float32)
                value_t[:, pl.ds(start, BLOCK)] = value.T.astype(jnp.bfloat16)
        key_seq[pl.ds(WINDOW, BLOCK), :] = jnp.zeros((BLOCK, HEAD_SIZE), jnp.bfloat16)
        value_t[:, pl.ds(WINDOW, BLOCK)] = jnp.zeros((HEAD_SIZE, BLOCK), jnp.bfloat16)

    first_block = scal_ref[WINDOW_BLOCKS + step]
    low_block = scal_ref[WINDOW_BLOCKS + CELL_BLOCKS + step]
    chunks = lax.shift_right_logical(first_block - low_block + 2, 1)
    top[...] = jnp.full_like(top, NEG_BIG)
    acc[...] = jnp.zeros_like(acc)

    def score_chunk(turn, _):
        key_start = pl.multiple_of((low_block + 2 * turn) * BLOCK, BLOCK)
        keys = key_seq[pl.ds(key_start, CHUNK), :]
        for tile in range(ROWS // TILE):
            cols = pl.ds(tile * TILE, TILE)
            queries = q_ref[tile // 2, pl.ds((tile % 2) * TILE, TILE), :]
            raw = dot(keys, queries, NT)
            allowed = allowed_tile(key_start, doc_ref[0, :, cols], row_positions(first_block, tile))
            raw = jnp.where(allowed, raw, NEG_BIG)
            scores[pl.ds(pl.multiple_of(turn * CHUNK, CHUNK), CHUNK), cols] = raw
            part = jnp.max(raw.reshape(CHUNK // 8, 8, TILE), axis=0)
            top[:, cols] = jnp.maximum(top[:, cols], part)
        return 0

    lax.fori_loop(0, chunks, score_chunk, 0)
    highest = jnp.max(top[...], axis=0, keepdims=True) * EXP2_SCALE
    top[...] = jnp.zeros_like(top)

    def value_chunk(turn, _):
        key_start = pl.multiple_of((low_block + 2 * turn) * BLOCK, BLOCK)
        values = value_t[:, pl.ds(key_start, CHUNK)]
        for tile in range(ROWS // TILE):
            cols = pl.ds(tile * TILE, TILE)
            raw = scores[pl.ds(pl.multiple_of(turn * CHUNK, CHUNK), CHUNK), cols]
            weights = jnp.exp2(raw * EXP2_SCALE - highest[:, tile * TILE : (tile + 1) * TILE])
            top[:, cols] += jnp.sum(weights.reshape(CHUNK // 8, 8, TILE), axis=0)
            acc[:, cols] += dot(values, weights.astype(jnp.bfloat16))
        return 0

    lax.fori_loop(0, chunks, value_chunk, 0)
    total = jnp.sum(top[...], axis=0, keepdims=True)
    lse_ref[0] = highest + jnp.log2(total)
    out_t = acc[...] * (1.0 / total)
    out_t_ref[0] = out_t.astype(jnp.bfloat16)
    out = out_t.T.astype(jnp.bfloat16)
    out_ref[0] = out[: ROWS // 2]
    out_ref[1] = out[ROWS // 2 :]


def backward_kernel(scal_ref, q_ref, grad_ref, out_t_ref, lse_ref, doc_ref, kv0_ref, kv1_ref, kv2_ref, dq_ref, dkv0_ref, dkv1_ref, dkv2_ref, key_seq, value_seq, key_t, dk_acc, dv_acc, dq_t, weights_low, grads_low, delta):
    step = pl.program_id(0)

    @pl.when(step == 0)
    def _():
        for slot, kv_ref in enumerate((kv0_ref, kv1_ref, kv2_ref)):
            for block in range(CELL_BLOCKS):
                start = window_start(scal_ref, slot, block)
                key = stored_rows(kv_ref, block, 0)
                key_seq[pl.ds(start, BLOCK), :] = key
                key_t[:, pl.ds(start, BLOCK)] = key.astype(jnp.float32).T.astype(jnp.bfloat16)
                value_seq[pl.ds(start, BLOCK), :] = stored_rows(kv_ref, block, 1)
        zeros = jnp.zeros((BLOCK, HEAD_SIZE), jnp.bfloat16)
        key_seq[pl.ds(WINDOW, BLOCK), :] = zeros
        value_seq[pl.ds(WINDOW, BLOCK), :] = zeros
        key_t[:, pl.ds(WINDOW, BLOCK)] = zeros
        dk_acc[...] = jnp.zeros_like(dk_acc)
        dv_acc[...] = jnp.zeros_like(dv_acc)

    first_block = scal_ref[WINDOW_BLOCKS + step]
    low_block = scal_ref[WINDOW_BLOCKS + CELL_BLOCKS + step]
    chunks = lax.shift_right_logical(first_block - low_block + 2, 1)
    dq_t[...] = jnp.zeros_like(dq_t)
    for half in range(2):
        cols = slice(half * ROWS // 2, (half + 1) * ROWS // 2)
        grad_t = grad_ref[half].astype(jnp.float32).T
        delta[:, cols] = jnp.sum(grad_t * out_t_ref[0, :, cols].astype(jnp.float32), axis=0, keepdims=True)

    def chunk(turn, _):
        key_start = pl.multiple_of((low_block + 2 * turn) * BLOCK, BLOCK)
        keys = key_seq[pl.ds(key_start, CHUNK), :]
        values = value_seq[pl.ds(key_start, CHUNK), :]
        for tile in range(ROWS // TILE):
            cols = pl.ds(tile * TILE, TILE)
            half, rows = tile // 2, pl.ds((tile % 2) * TILE, TILE)
            raw = dot(keys, q_ref[half, rows, :], NT)
            allowed = allowed_tile(key_start, doc_ref[0, :, cols], row_positions(first_block, tile))
            weights = jnp.exp2(jnp.where(allowed, raw * EXP2_SCALE - lse_ref[0, :, cols], NEG_BIG))
            weights_low[:, cols] = weights.astype(jnp.bfloat16)
            sent = dot(values, grad_ref[half, rows, :], NT)
            grads = (weights * (sent - delta[:, cols])).astype(jnp.bfloat16)
            grads_low[:, cols] = grads
            dq_t[:, cols] += dot(key_t[:, pl.ds(key_start, CHUNK)], grads)
        queries = jnp.concatenate([q_ref[0], q_ref[1]], axis=0)
        out_grads = jnp.concatenate([grad_ref[0], grad_ref[1]], axis=0)
        dk_acc[pl.ds(key_start, CHUNK), :] += dot(grads_low[...], queries)
        dv_acc[pl.ds(key_start, CHUNK), :] += dot(weights_low[...], out_grads)
        return 0

    lax.fori_loop(0, chunks, chunk, 0)
    query_grad = (dq_t[...] * SCALE).T.astype(jnp.bfloat16)
    dq_ref[0] = query_grad[: ROWS // 2]
    dq_ref[1] = query_grad[ROWS // 2 :]

    @pl.when(step == CELL_BLOCKS - 1)
    def _():
        for slot, dkv_ref in enumerate((dkv0_ref, dkv1_ref, dkv2_ref)):
            for block in range(CELL_BLOCKS):
                start = window_start(scal_ref, slot, block)
                dk = (dk_acc[pl.ds(start, BLOCK), :] * SCALE).astype(jnp.bfloat16)
                dv = dv_acc[pl.ds(start, BLOCK), :].astype(jnp.bfloat16)
                for half in range(2):
                    rows = slice(half * 64, (half + 1) * 64)
                    dkv_ref[2 * block + half, pl.ds(0, 64), :] = dk[rows]
                    dkv_ref[2 * block + half, pl.ds(64, 64), :] = dv[rows]


def row_spec():
    return pl.BlockSpec((2, ROWS // 2, HEAD_SIZE), lambda b, s: (b, 0, 0))


def lane_spec(rows):
    return pl.BlockSpec((1, rows, ROWS), lambda b, s: (b, 0, 0))


def kv_spec():
    return pl.BlockSpec((8, 128, HEAD_SIZE), lambda b, s: (0, 0, 0))


def params():
    return pltpu.CompilerParams(dimension_semantics=("arbitrary",), vmem_limit_bytes=60 * 1024 * 1024)


def forward(scal, q_in, doc_rows, kv):
    return pl.pallas_call(
        forward_kernel,
        grid_spec=pltpu.PrefetchScalarGridSpec(
            num_scalar_prefetch=1,
            grid=(CELL_BLOCKS,),
            in_specs=[row_spec(), lane_spec(1), kv_spec(), kv_spec(), kv_spec()],
            out_specs=[row_spec(), lane_spec(HEAD_SIZE), lane_spec(1)],
            scratch_shapes=[
                pltpu.VMEM((PADDED, HEAD_SIZE), jnp.bfloat16),
                pltpu.VMEM((HEAD_SIZE, PADDED), jnp.bfloat16),
                pltpu.VMEM((REACH, ROWS), jnp.float32),
                pltpu.VMEM((HEAD_SIZE, ROWS), jnp.float32),
                pltpu.VMEM((8, ROWS), jnp.float32),
            ],
        ),
        out_shape=[
            jax.ShapeDtypeStruct((8, ROWS // 2, HEAD_SIZE), jnp.bfloat16),
            jax.ShapeDtypeStruct((CELL_BLOCKS, HEAD_SIZE, ROWS), jnp.bfloat16),
            jax.ShapeDtypeStruct((CELL_BLOCKS, 1, ROWS), jnp.float32),
        ],
        compiler_params=params(),
        cost_estimate=pl.CostEstimate(flops=4_000_000_000, bytes_accessed=4_000_000, transcendentals=4_000_000),
        name="forward",
    )(scal, q_in, doc_rows, *kv)


def backward(scal, q_in, grad_in, out_t, lse, doc_rows, kv):
    dkv_shape = jax.ShapeDtypeStruct((8, 128, HEAD_SIZE), jnp.bfloat16)
    return pl.pallas_call(
        backward_kernel,
        grid_spec=pltpu.PrefetchScalarGridSpec(
            num_scalar_prefetch=1,
            grid=(CELL_BLOCKS,),
            in_specs=[row_spec(), row_spec(), lane_spec(HEAD_SIZE), lane_spec(1), lane_spec(1), kv_spec(), kv_spec(), kv_spec()],
            out_specs=[row_spec(), kv_spec(), kv_spec(), kv_spec()],
            scratch_shapes=[
                pltpu.VMEM((PADDED, HEAD_SIZE), jnp.bfloat16),
                pltpu.VMEM((PADDED, HEAD_SIZE), jnp.bfloat16),
                pltpu.VMEM((HEAD_SIZE, PADDED), jnp.bfloat16),
                pltpu.VMEM((PADDED, HEAD_SIZE), jnp.float32),
                pltpu.VMEM((PADDED, HEAD_SIZE), jnp.float32),
                pltpu.VMEM((HEAD_SIZE, ROWS), jnp.float32),
                pltpu.VMEM((CHUNK, ROWS), jnp.bfloat16),
                pltpu.VMEM((CHUNK, ROWS), jnp.bfloat16),
                pltpu.VMEM((1, ROWS), jnp.float32),
            ],
        ),
        out_shape=[jax.ShapeDtypeStruct((8, ROWS // 2, HEAD_SIZE), jnp.bfloat16), dkv_shape, dkv_shape, dkv_shape],
        compiler_params=params(),
        cost_estimate=pl.CostEstimate(flops=10_000_000_000, bytes_accessed=6_000_000, transcendentals=4_000_000),
        name="backward",
    )(scal, q_in, grad_in, out_t, lse, doc_rows, *kv)


def by_head(rows):
    tokens = rows.shape[0]
    split = rows.reshape(tokens, 8, -1, HEAD_SIZE).transpose(1, 0, 2, 3)
    return split.reshape(8, -1, HEAD_SIZE)


def exchanged(block):
    return lax.all_to_all(block, "head", split_axis=0, concat_axis=0, tiled=True)


def plan(doc_lengths, stored_block_order):
    cell = lax.axis_index("ctx")
    starts = jnp.cumsum(doc_lengths) - doc_lengths
    window_first = (cell - (SLOTS - 1)) * CELL_BLOCKS
    padded = jnp.pad(stored_block_order, (WINDOW_BLOCKS - CELL_BLOCKS, 0))
    window_order = lax.dynamic_slice_in_dim(padded, cell * CELL_BLOCKS, WINDOW_BLOCKS, 0)
    base = jnp.arange(WINDOW_BLOCKS, dtype=jnp.int32) // CELL_BLOCKS * CELL_BLOCKS
    place = base + window_order % CELL_BLOCKS
    own_place = place[WINDOW_BLOCKS - CELL_BLOCKS :]
    own_block = window_first + own_place
    token = lax.broadcasted_iota(jnp.int32, (CELL_BLOCKS, 1, ROWS), 2) // SHARE
    pos = own_block[:, None, None] * BLOCK + token
    begun = starts <= pos[..., None]
    doc_start = jnp.max(jnp.where(begun, starts, 0), axis=-1)
    doc_rows = doc_start - window_first * BLOCK
    low = jnp.max(jnp.where(starts <= own_block[:, None] * BLOCK, starts, 0), axis=-1)
    low_block = low // BLOCK - window_first
    scal = jnp.concatenate([place, own_place, low_block]).astype(jnp.int32)
    return scal, doc_rows.astype(jnp.int32)


def body(queries, keys, values, out_grad, doc_lengths, stored_block_order):
    scal, doc_rows = plan(doc_lengths, stored_block_order)
    kv0 = exchanged(jnp.concatenate([by_head(keys), by_head(values)], axis=1))
    q_in = exchanged(by_head(queries))
    kv1 = passed_along(kv0, "ctx", 1)
    kv2 = passed_along(kv1, "ctx", 1)
    grad_rows, kv2 = lax.optimization_barrier((by_head(out_grad), kv2))
    grad_in = exchanged(grad_rows)
    kv = (kv0, kv1, kv2)
    attended_loc, out_t, lse = forward(scal, q_in, doc_rows, kv)
    attended_in = exchanged(attended_loc)
    query_grad_loc, dkv0, dkv1, dkv2 = backward(scal, q_in, grad_in, out_t, lse, doc_rows, kv)
    attended_in, dkv2, query_grad_loc = lax.optimization_barrier((attended_in, dkv2, query_grad_loc))
    query_grad_in = exchanged(query_grad_loc)
    carried = passed_along(dkv2, "ctx", -1).astype(jnp.float32) + dkv1.astype(jnp.float32)
    carried = passed_along(carried.astype(jnp.bfloat16), "ctx", -1).astype(jnp.float32) + dkv0.astype(jnp.float32)
    carried, query_grad_in = lax.optimization_barrier((carried.astype(jnp.bfloat16), query_grad_in))
    dkv_in = exchanged(carried)
    tokens = queries.shape[0]

    def by_token(block, heads):
        return block.reshape(8, tokens, heads, HEAD_SIZE).transpose(1, 0, 2, 3).reshape(tokens, -1, HEAD_SIZE)

    attended = by_token(attended_in, SHARE)
    query_grad = by_token(query_grad_in, SHARE)
    key_gradient = by_token(dkv_in[:, :64], 1)
    value_gradient = by_token(dkv_in[:, 64:], 1)
    return attended, query_grad, key_gradient, value_gradient


def solution(mesh):
    spec = P(("ctx", "head"), None, None)
    return jax.shard_map(
        body,
        mesh=mesh,
        in_specs=(spec, spec, spec, spec, P(), P()),
        out_specs=(spec, spec, spec, spec),
        check_vma=False,
    )
```

```python
import functools
import math

import jax
import jax.numpy as jnp
from jax import lax
from jax.experimental import pallas as pl
from jax.experimental.pallas import tpu as pltpu
from jax.sharding import PartitionSpec as P

HEAD_SIZE = 128
BLOCK = 128
CELL_BLOCKS = 4
SLOTS = 3
WINDOW_BLOCKS = SLOTS * CELL_BLOCKS
WINDOW = WINDOW_BLOCKS * BLOCK
CHUNK = 2 * BLOCK
PADDED = WINDOW + BLOCK
REACH = 10 * BLOCK
SHARE = 8
ROWS = BLOCK * SHARE
TILE = ROWS // 2

SCALE = HEAD_SIZE ** (-0.5)
EXP2_SCALE = SCALE * math.log2(math.e)
NEG_BIG = -1e30

NT = (((1,), (1,)), ((), ()))
NN = (((1,), (0,)), ((), ()))
TN = (((0,), (0,)), ((), ()))


def dot(a, b, dims=NN):
    return lax.dot_general(a, b, dims, preferred_element_type=jnp.float32)


def passed_along(block, axis, distance):
    devices = range(lax.axis_size(axis))
    route = [(i - distance, i) for i in devices if i - distance in devices]
    return lax.ppermute(block, axis, route)


def stored_rows(kv_ref, block, which):
    first = kv_ref[2 * block, pl.ds(64 * which, 64), :]
    second = kv_ref[2 * block + 1, pl.ds(64 * which, 64), :]
    return jnp.concatenate([first, second], axis=0)


def window_start(scal_ref, slot, block):
    index = (SLOTS - 1 - slot) * CELL_BLOCKS + block
    return pl.multiple_of(scal_ref[index] * BLOCK, BLOCK)


def allowed_tile(key_start, first_block, doc_start, tile):
    lane = lax.broadcasted_iota(jnp.int32, (1, TILE), 1) + tile * TILE
    query_pos = first_block * BLOCK + lax.shift_right_logical(lane, 3)
    key_pos = lax.broadcasted_iota(jnp.int32, (CHUNK, TILE), 0)
    return (key_pos >= doc_start - key_start) & (key_pos <= query_pos - key_start)


def each_chunk(scal_ref, step, work):
    first_block = scal_ref[WINDOW_BLOCKS + step]
    low_block = scal_ref[WINDOW_BLOCKS + CELL_BLOCKS + step]
    last_start = scal_ref[WINDOW_BLOCKS + 2 * CELL_BLOCKS + step]
    chunks = lax.shift_right_logical(first_block - low_block + 2, 1)

    def turn_work(turn, _):
        key_start = pl.multiple_of((low_block + 2 * turn) * BLOCK, BLOCK)
        whole = (key_start >= last_start) & (key_start + CHUNK <= first_block * BLOCK)

        @pl.when(whole)
        def _():
            work(turn, key_start, first_block, False)

        @pl.when(jnp.logical_not(whole))
        def _():
            work(turn, key_start, first_block, True)

        return 0

    lax.fori_loop(0, chunks, turn_work, 0)


def forward_kernel(scal_ref, q_ref, doc_ref, kv0_ref, kv1_ref, kv2_ref, out_ref, out_t_ref, lse_ref, key_seq, value_t, scores, acc, top):
    step = pl.program_id(0)

    @pl.when(step == 0)
    def _():
        for slot, kv_ref in enumerate((kv0_ref, kv1_ref, kv2_ref)):
            for block in range(CELL_BLOCKS):
                start = window_start(scal_ref, slot, block)
                key_seq[pl.ds(start, BLOCK), :] = stored_rows(kv_ref, block, 0)
                value = stored_rows(kv_ref, block, 1).astype(jnp.float32)
                value_t[:, pl.ds(start, BLOCK)] = value.T.astype(jnp.bfloat16)
        key_seq[pl.ds(WINDOW, BLOCK), :] = jnp.zeros((BLOCK, HEAD_SIZE), jnp.bfloat16)
        value_t[:, pl.ds(WINDOW, BLOCK)] = jnp.zeros((HEAD_SIZE, BLOCK), jnp.bfloat16)

    top[...] = jnp.full_like(top, NEG_BIG)
    acc[...] = jnp.zeros_like(acc)

    def score_chunk(turn, key_start, first_block, masked):
        keys = key_seq[pl.ds(key_start, CHUNK), :]
        rows = pl.ds(pl.multiple_of(turn * CHUNK, CHUNK), CHUNK)
        for tile in range(2):
            cols = slice(tile * TILE, (tile + 1) * TILE)
            raw = dot(keys, q_ref[tile], NT)
            if masked:
                raw = jnp.where(allowed_tile(key_start, first_block, doc_ref[0, :, cols], tile), raw, NEG_BIG)
            scores[rows, cols] = raw
            part = jnp.max(raw.reshape(CHUNK // 8, 8, TILE), axis=0)
            top[:, cols] = jnp.maximum(top[:, cols], part)

    each_chunk(scal_ref, step, score_chunk)
    highest = jnp.max(top[...], axis=0, keepdims=True) * EXP2_SCALE
    top[...] = jnp.zeros_like(top)
    first_block = scal_ref[WINDOW_BLOCKS + step]
    low_block = scal_ref[WINDOW_BLOCKS + CELL_BLOCKS + step]

    def value_chunk(turn, _):
        key_start = pl.multiple_of((low_block + 2 * turn) * BLOCK, BLOCK)
        rows = pl.ds(pl.multiple_of(turn * CHUNK, CHUNK), CHUNK)
        values = value_t[:, pl.ds(key_start, CHUNK)]
        for tile in range(2):
            cols = slice(tile * TILE, (tile + 1) * TILE)
            weights = jnp.exp2(scores[rows, cols] * EXP2_SCALE - highest[:, cols])
            top[:, cols] += jnp.sum(weights.reshape(CHUNK // 8, 8, TILE), axis=0)
            acc[:, cols] += dot(values, weights.astype(jnp.bfloat16))
        return 0

    lax.fori_loop(0, lax.shift_right_logical(first_block - low_block + 2, 1), value_chunk, 0)
    total = jnp.sum(top[...], axis=0, keepdims=True)
    lse_ref[0] = highest + jnp.log2(total)
    out_t = acc[...] * (1.0 / total)
    out_t_ref[0] = out_t.astype(jnp.bfloat16)
    out = out_t.T.astype(jnp.bfloat16)
    out_ref[0] = out[: ROWS // 2]
    out_ref[1] = out[ROWS // 2 :]


def backward_kernel(scal_ref, q_ref, grad_ref, out_t_ref, lse_ref, doc_ref, kv0_ref, kv1_ref, kv2_ref, dq_ref, dkv0_ref, dkv1_ref, dkv2_ref, key_seq, value_seq, dk_acc, dv_acc, dq_acc, weights_low, grads_low, delta):
    step = pl.program_id(0)

    @pl.when(step == 0)
    def _():
        for slot, kv_ref in enumerate((kv0_ref, kv1_ref, kv2_ref)):
            for block in range(CELL_BLOCKS):
                start = window_start(scal_ref, slot, block)
                key_seq[pl.ds(start, BLOCK), :] = stored_rows(kv_ref, block, 0)
                value_seq[pl.ds(start, BLOCK), :] = stored_rows(kv_ref, block, 1)
        zeros = jnp.zeros((BLOCK, HEAD_SIZE), jnp.bfloat16)
        key_seq[pl.ds(WINDOW, BLOCK), :] = zeros
        value_seq[pl.ds(WINDOW, BLOCK), :] = zeros
        dk_acc[...] = jnp.zeros_like(dk_acc)
        dv_acc[...] = jnp.zeros_like(dv_acc)

    dq_acc[...] = jnp.zeros_like(dq_acc)
    for half in range(2):
        cols = slice(half * TILE, (half + 1) * TILE)
        grad_t = grad_ref[half].astype(jnp.float32).T
        delta[:, cols] = jnp.sum(grad_t * out_t_ref[0, :, cols].astype(jnp.float32), axis=0, keepdims=True)

    def chunk(turn, key_start, first_block, masked):
        keys = key_seq[pl.ds(key_start, CHUNK), :]
        values = value_seq[pl.ds(key_start, CHUNK), :]
        for tile in range(2):
            cols = slice(tile * TILE, (tile + 1) * TILE)
            raw = dot(keys, q_ref[tile], NT)
            scaled = raw * EXP2_SCALE - lse_ref[0, :, cols]
            if masked:
                scaled = jnp.where(allowed_tile(key_start, first_block, doc_ref[0, :, cols], tile), scaled, NEG_BIG)
            weights = jnp.exp2(scaled)
            weights_low[:, cols] = weights.astype(jnp.bfloat16)
            sent = dot(values, grad_ref[tile], NT)
            grads_low[:, cols] = (weights * (sent - delta[:, cols])).astype(jnp.bfloat16)
        queries = jnp.concatenate([q_ref[0], q_ref[1]], axis=0)
        out_grads = jnp.concatenate([grad_ref[0], grad_ref[1]], axis=0)
        dq_acc[...] += dot(grads_low[...], keys, TN)
        dk_acc[pl.ds(key_start, CHUNK), :] += dot(grads_low[...], queries)
        dv_acc[pl.ds(key_start, CHUNK), :] += dot(weights_low[...], out_grads)

    each_chunk(scal_ref, step, chunk)
    query_grad = (dq_acc[...] * SCALE).astype(jnp.bfloat16)
    dq_ref[0] = query_grad[:TILE]
    dq_ref[1] = query_grad[TILE:]

    @pl.when(step == CELL_BLOCKS - 1)
    def _():
        for slot, dkv_ref in enumerate((dkv0_ref, dkv1_ref, dkv2_ref)):
            for block in range(CELL_BLOCKS):
                start = window_start(scal_ref, slot, block)
                dk = (dk_acc[pl.ds(start, BLOCK), :] * SCALE).astype(jnp.bfloat16)
                dv = dv_acc[pl.ds(start, BLOCK), :].astype(jnp.bfloat16)
                for half in range(2):
                    rows = slice(half * 64, (half + 1) * 64)
                    dkv_ref[2 * block + half, pl.ds(0, 64), :] = dk[rows]
                    dkv_ref[2 * block + half, pl.ds(64, 64), :] = dv[rows]


def row_spec():
    return pl.BlockSpec((2, ROWS // 2, HEAD_SIZE), lambda b, s: (b, 0, 0))


def lane_spec(rows):
    return pl.BlockSpec((1, rows, ROWS), lambda b, s: (b, 0, 0))


def kv_spec():
    return pl.BlockSpec((8, 128, HEAD_SIZE), lambda b, s: (0, 0, 0))


def params():
    return pltpu.CompilerParams(dimension_semantics=("arbitrary",), vmem_limit_bytes=60 * 1024 * 1024)


def forward(scal, q_in, doc_rows, kv):
    return pl.pallas_call(
        forward_kernel,
        grid_spec=pltpu.PrefetchScalarGridSpec(
            num_scalar_prefetch=1,
            grid=(CELL_BLOCKS,),
            in_specs=[row_spec(), lane_spec(1), kv_spec(), kv_spec(), kv_spec()],
            out_specs=[row_spec(), lane_spec(HEAD_SIZE), lane_spec(1)],
            scratch_shapes=[
                pltpu.VMEM((PADDED, HEAD_SIZE), jnp.bfloat16),
                pltpu.VMEM((HEAD_SIZE, PADDED), jnp.bfloat16),
                pltpu.VMEM((REACH, ROWS), jnp.float32),
                pltpu.VMEM((HEAD_SIZE, ROWS), jnp.float32),
                pltpu.VMEM((8, ROWS), jnp.float32),
            ],
        ),
        out_shape=[
            jax.ShapeDtypeStruct((8, ROWS // 2, HEAD_SIZE), jnp.bfloat16),
            jax.ShapeDtypeStruct((CELL_BLOCKS, HEAD_SIZE, ROWS), jnp.bfloat16),
            jax.ShapeDtypeStruct((CELL_BLOCKS, 1, ROWS), jnp.float32),
        ],
        compiler_params=params(),
        cost_estimate=pl.CostEstimate(flops=4_000_000_000, bytes_accessed=4_000_000, transcendentals=4_000_000),
        name="forward",
    )(scal, q_in, doc_rows, *kv)


def backward(scal, q_in, grad_in, out_t, lse, doc_rows, kv):
    dkv_shape = jax.ShapeDtypeStruct((8, 128, HEAD_SIZE), jnp.bfloat16)
    return pl.pallas_call(
        backward_kernel,
        grid_spec=pltpu.PrefetchScalarGridSpec(
            num_scalar_prefetch=1,
            grid=(CELL_BLOCKS,),
            in_specs=[row_spec(), row_spec(), lane_spec(HEAD_SIZE), lane_spec(1), lane_spec(1), kv_spec(), kv_spec(), kv_spec()],
            out_specs=[row_spec(), kv_spec(), kv_spec(), kv_spec()],
            scratch_shapes=[
                pltpu.VMEM((PADDED, HEAD_SIZE), jnp.bfloat16),
                pltpu.VMEM((PADDED, HEAD_SIZE), jnp.bfloat16),
                pltpu.VMEM((PADDED, HEAD_SIZE), jnp.float32),
                pltpu.VMEM((PADDED, HEAD_SIZE), jnp.float32),
                pltpu.VMEM((ROWS, HEAD_SIZE), jnp.float32),
                pltpu.VMEM((CHUNK, ROWS), jnp.bfloat16),
                pltpu.VMEM((CHUNK, ROWS), jnp.bfloat16),
                pltpu.VMEM((1, ROWS), jnp.float32),
            ],
        ),
        out_shape=[jax.ShapeDtypeStruct((8, ROWS // 2 + 128, HEAD_SIZE), jnp.bfloat16), dkv_shape, dkv_shape, dkv_shape],
        compiler_params=params(),
        cost_estimate=pl.CostEstimate(flops=10_000_000_000, bytes_accessed=6_000_000, transcendentals=4_000_000),
        name="backward",
    )(scal, q_in, grad_in, out_t, lse, doc_rows, *kv)


def by_head(rows):
    tokens = rows.shape[0]
    split = rows.reshape(tokens, 8, -1, HEAD_SIZE).transpose(1, 0, 2, 3)
    return split.reshape(8, -1, HEAD_SIZE)


def exchanged(block):
    return lax.all_to_all(block, "head", split_axis=0, concat_axis=0, tiled=True)


def plan(doc_lengths, stored_block_order):
    cell = lax.axis_index("ctx")
    starts = jnp.cumsum(doc_lengths) - doc_lengths
    window_first = (cell - (SLOTS - 1)) * CELL_BLOCKS
    padded = jnp.pad(stored_block_order, (WINDOW_BLOCKS - CELL_BLOCKS, 0))
    window_order = lax.dynamic_slice_in_dim(padded, cell * CELL_BLOCKS, WINDOW_BLOCKS, 0)
    base = jnp.arange(WINDOW_BLOCKS, dtype=jnp.int32) // CELL_BLOCKS * CELL_BLOCKS
    place = base + window_order % CELL_BLOCKS
    own_place = place[WINDOW_BLOCKS - CELL_BLOCKS :]
    own_block = window_first + own_place
    token = lax.broadcasted_iota(jnp.int32, (CELL_BLOCKS, 1, ROWS), 2) // SHARE
    pos = own_block[:, None, None] * BLOCK + token
    begun = starts <= pos[..., None]
    doc_start = jnp.max(jnp.where(begun, starts, 0), axis=-1)
    doc_rows = doc_start - window_first * BLOCK
    edges = jnp.concatenate([own_block * BLOCK, own_block * BLOCK + BLOCK - 1])
    low = jnp.max(jnp.where(starts <= edges[:, None], starts, 0), axis=-1) - window_first * BLOCK
    scal = jnp.concatenate([place, own_place, low[:CELL_BLOCKS] // BLOCK, low[CELL_BLOCKS:]]).astype(jnp.int32)
    return scal, doc_rows.astype(jnp.int32)


def body(queries, keys, values, out_grad, doc_lengths, stored_block_order):
    scal, doc_rows = plan(doc_lengths, stored_block_order)
    first_in = exchanged(jnp.concatenate([by_head(queries), by_head(keys), by_head(values)], axis=1))
    kv0 = first_in[:, 512:, :]
    kv = (kv0, passed_along(kv0, "ctx", 1), passed_along(kv0, "ctx", 2))
    grad_in = exchanged(by_head(out_grad))
    attended_loc, out_t, lse = forward(scal, first_in, doc_rows, kv)
    attended_in = exchanged(attended_loc)
    last_loc, dkv0, dkv1, dkv2 = backward(scal, first_in, grad_in, out_t, lse, doc_rows, kv)
    attended_in, dkv1, dkv2 = lax.optimization_barrier((attended_in, dkv1, dkv2))
    near, far = passed_along(dkv1, "ctx", -1), passed_along(dkv2, "ctx", -2)
    summed = dkv0.astype(jnp.float32) + near.astype(jnp.float32) + far.astype(jnp.float32)
    last_loc = lax.dynamic_update_slice(last_loc, summed.astype(jnp.bfloat16), (0, 512, 0))
    last_in = exchanged(last_loc)
    tokens = queries.shape[0]

    def by_token(block, heads):
        return block.reshape(8, tokens, heads, HEAD_SIZE).transpose(1, 0, 2, 3).reshape(tokens, -1, HEAD_SIZE)

    attended = by_token(attended_in, SHARE)
    query_grad = by_token(last_in[:, :512], SHARE)
    key_gradient = by_token(last_in[:, 512:576], 1)
    value_gradient = by_token(last_in[:, 576:], 1)
    return attended, query_grad, key_gradient, value_gradient


def solution(mesh):
    spec = P(("ctx", "head"), None, None)
    return jax.shard_map(
        body,
        mesh=mesh,
        in_specs=(spec, spec, spec, spec, P(), P()),
        out_specs=(spec, spec, spec, spec),
        check_vma=False,
    )
```

```python
import functools
import math

import jax
import jax.numpy as jnp
from jax import lax
from jax.experimental import pallas as pl
from jax.experimental.pallas import tpu as pltpu
from jax.sharding import PartitionSpec as P

HEAD_SIZE = 128
BLOCK = 128
CELL_BLOCKS = 4
SLOTS = 3
WINDOW_BLOCKS = SLOTS * CELL_BLOCKS
WINDOW = WINDOW_BLOCKS * BLOCK
CHUNK = 2 * BLOCK
PADDED = WINDOW + BLOCK
REACH = 10 * BLOCK
SHARE = 8
PARTS = 2
PART_TOKENS = 64 // PARTS
PART_ROWS = PART_TOKENS * SHARE
ROWS = 2 * PART_ROWS

SCALE = HEAD_SIZE ** (-0.5)
EXP2_SCALE = SCALE * math.log2(math.e)
NEG_BIG = -1e30

NT = (((1,), (1,)), ((), ()))
NN = (((1,), (0,)), ((), ()))
TN = (((0,), (0,)), ((), ()))


def dot(a, b, dims=NN):
    return lax.dot_general(a, b, dims, preferred_element_type=jnp.float32)


def passed_along(block, axis, distance):
    devices = range(lax.axis_size(axis))
    route = [(i - distance, i) for i in devices if i - distance in devices]
    return lax.ppermute(block, axis, route)


def stored_rows(kv_ref, block, which):
    first = kv_ref[2 * block, pl.ds(64 * which, 64), :]
    second = kv_ref[2 * block + 1, pl.ds(64 * which, 64), :]
    return jnp.concatenate([first, second], axis=0)


def window_start(scal_ref, slot, block):
    index = (SLOTS - 1 - slot) * CELL_BLOCKS + block
    return pl.multiple_of(scal_ref[index] * BLOCK, BLOCK)


def allowed_tile(key_start, first_block, doc_start, part):
    lane = lax.broadcasted_iota(jnp.int32, (1, ROWS), 1)
    token = jnp.where(lane >= PART_ROWS, 64 - PART_TOKENS, 0) + lax.shift_right_logical(lane, 3)
    query_pos = first_block * BLOCK + part * PART_TOKENS + token
    key_pos = lax.broadcasted_iota(jnp.int32, (CHUNK, ROWS), 0)
    return (key_pos >= doc_start - key_start) & (key_pos <= query_pos - key_start)


def each_chunk(low_block, chunks, work):
    def turn_work(turn, _):
        key_start = pl.multiple_of((low_block + 2 * turn) * BLOCK, BLOCK)
        work(turn, key_start, pl.ds(pl.multiple_of(turn * CHUNK, CHUNK), CHUNK))
        return 0

    lax.fori_loop(0, chunks, turn_work, 0)


def attention_kernel(part, scal_ref, q_ref, grad_ref, doc_ref, kv0_ref, kv1_ref, kv2_ref, *refs):
    if part == 0:
        out_ref, dk_acc, dv_acc, *scratch = refs
    else:
        dk_in, dv_in, out_ref, dkv0_ref, dkv1_ref, dkv2_ref, dk_acc, dv_acc, *scratch = refs
    key_seq, value_seq, value_t, scores, acc, top, dq_acc = scratch
    step = pl.program_id(0)

    @pl.when(step == 0)
    def _():
        for slot, kv_ref in enumerate((kv0_ref, kv1_ref, kv2_ref)):
            for block in range(CELL_BLOCKS):
                start = window_start(scal_ref, slot, block)
                key_seq[pl.ds(start, BLOCK), :] = stored_rows(kv_ref, block, 0)
                value = stored_rows(kv_ref, block, 1)
                value_seq[pl.ds(start, BLOCK), :] = value
                value_t[:, pl.ds(start, BLOCK)] = value.astype(jnp.float32).T.astype(jnp.bfloat16)
        zeros = jnp.zeros((BLOCK, HEAD_SIZE), jnp.bfloat16)
        key_seq[pl.ds(WINDOW, BLOCK), :] = zeros
        value_seq[pl.ds(WINDOW, BLOCK), :] = zeros
        value_t[:, pl.ds(WINDOW, BLOCK)] = zeros
        if part == 0:
            dk_acc[...] = jnp.zeros_like(dk_acc)
            dv_acc[...] = jnp.zeros_like(dv_acc)
        else:
            dk_acc[...] = dk_in[...]
            dv_acc[...] = dv_in[...]

    first_block = scal_ref[WINDOW_BLOCKS + step]
    low_block = scal_ref[WINDOW_BLOCKS + CELL_BLOCKS + step]
    last_start = scal_ref[WINDOW_BLOCKS + 2 * CELL_BLOCKS + step]
    chunks = lax.shift_right_logical(first_block - low_block + 2, 1)
    queries = q_ref[...].reshape(ROWS, HEAD_SIZE)
    out_grads = grad_ref[...].reshape(ROWS, HEAD_SIZE)
    top[...] = jnp.full_like(top, NEG_BIG)
    acc[...] = jnp.zeros_like(acc)
    dq_acc[...] = jnp.zeros_like(dq_acc)

    def score_chunk(turn, key_start, rows):
        def score(masked):
            raw = dot(key_seq[pl.ds(key_start, CHUNK), :], queries, NT)
            if masked:
                raw = jnp.where(allowed_tile(key_start, first_block, doc_ref[0], part), raw, NEG_BIG)
            scores[rows, :] = raw
            top[...] = jnp.maximum(top[...], jnp.max(raw.reshape(CHUNK // 8, 8, ROWS), axis=0))

        whole = (key_start >= last_start) & (key_start + CHUNK <= first_block * BLOCK)
        pl.when(whole)(lambda: score(False))
        pl.when(jnp.logical_not(whole))(lambda: score(True))

    each_chunk(low_block, chunks, score_chunk)
    highest = jnp.max(top[...], axis=0, keepdims=True) * EXP2_SCALE
    top[...] = jnp.zeros_like(top)

    def value_chunk(turn, key_start, rows):
        weights = jnp.exp2(scores[rows, :] * EXP2_SCALE - highest)
        top[...] += jnp.sum(weights.reshape(CHUNK // 8, 8, ROWS), axis=0)
        acc[...] += dot(value_t[:, pl.ds(key_start, CHUNK)], weights.astype(jnp.bfloat16))

    each_chunk(low_block, chunks, value_chunk)
    total = jnp.sum(top[...], axis=0, keepdims=True)
    lse = highest + jnp.log2(total)
    out = (acc[...] * (1.0 / total)).T.astype(jnp.bfloat16)
    out_ref[:, :PART_ROWS, :] = out.reshape(2, PART_ROWS, HEAD_SIZE)
    delta = jnp.sum((out.astype(jnp.float32) * out_grads.astype(jnp.float32)).T, axis=0, keepdims=True)

    def grad_chunk(turn, key_start, rows):
        window = pl.ds(key_start, CHUNK)
        weights = jnp.exp2(scores[rows, :] * EXP2_SCALE - lse)
        sent = dot(value_seq[window, :], out_grads, NT)
        grads = (weights * (sent - delta)).astype(jnp.bfloat16)
        dq_acc[...] += dot(grads, key_seq[window, :], TN)
        dk_acc[window, :] += dot(grads, queries)
        dv_acc[window, :] += dot(weights.astype(jnp.bfloat16), out_grads)

    each_chunk(low_block, chunks, grad_chunk)
    query_grad = (dq_acc[...] * SCALE).astype(jnp.bfloat16)
    out_ref[:, PART_ROWS:, :] = query_grad.reshape(2, PART_ROWS, HEAD_SIZE)

    if part == 1:

        @pl.when(step == CELL_BLOCKS - 1)
        def _():
            for slot, dkv_ref in enumerate((dkv0_ref, dkv1_ref, dkv2_ref)):
                for block in range(CELL_BLOCKS):
                    start = window_start(scal_ref, slot, block)
                    dk = (dk_acc[pl.ds(start, BLOCK), :] * SCALE).astype(jnp.bfloat16)
                    dv = dv_acc[pl.ds(start, BLOCK), :].astype(jnp.bfloat16)
                    for half in range(2):
                        rows = slice(half * 64, (half + 1) * 64)
                        dkv_ref[2 * block + half, pl.ds(0, 64), :] = dk[rows]
                        dkv_ref[2 * block + half, pl.ds(64, 64), :] = dv[rows]


def attention(part, scal, rows_in, doc_rows, kv, sums=()):
    def resident(shape):
        return pl.BlockSpec(shape, lambda b, s: (0,) * len(shape))

    def row_spec(place):
        return pl.BlockSpec((2, PART_ROWS, HEAD_SIZE), lambda b, s: (b, place, 0))

    kv_spec = resident((8, 128, HEAD_SIZE))
    sum_spec = resident((PADDED, HEAD_SIZE))
    sum_shape = jax.ShapeDtypeStruct((PADDED, HEAD_SIZE), jnp.float32)
    out_rows = 2 * PART_ROWS + (128 if part else 0)
    out_specs = [pl.BlockSpec((2, 2 * PART_ROWS, HEAD_SIZE), lambda b, s: (b, 0, 0))]
    out_shape = [jax.ShapeDtypeStruct((8, out_rows, HEAD_SIZE), jnp.bfloat16)]
    scratch = [
        pltpu.VMEM((PADDED, HEAD_SIZE), jnp.bfloat16),
        pltpu.VMEM((PADDED, HEAD_SIZE), jnp.bfloat16),
        pltpu.VMEM((HEAD_SIZE, PADDED), jnp.bfloat16),
        pltpu.VMEM((REACH, ROWS), jnp.float32),
        pltpu.VMEM((HEAD_SIZE, ROWS), jnp.float32),
        pltpu.VMEM((8, ROWS), jnp.float32),
        pltpu.VMEM((ROWS, HEAD_SIZE), jnp.float32),
    ]
    if part == 0:
        out_specs += [sum_spec, sum_spec]
        out_shape += [sum_shape, sum_shape]
    else:
        out_specs += [kv_spec] * 3
        out_shape += [jax.ShapeDtypeStruct((8, 128, HEAD_SIZE), jnp.bfloat16)] * 3
        scratch = [pltpu.VMEM((PADDED, HEAD_SIZE), jnp.float32)] * 2 + scratch
    return pl.pallas_call(
        functools.partial(attention_kernel, part),
        grid_spec=pltpu.PrefetchScalarGridSpec(
            num_scalar_prefetch=1,
            grid=(CELL_BLOCKS,),
            in_specs=[row_spec(0), row_spec(1), pl.BlockSpec((1, 1, ROWS), lambda b, s: (b, 0, 0))] + [kv_spec] * 3 + [sum_spec] * len(sums),
            out_specs=out_specs,
            scratch_shapes=scratch,
        ),
        out_shape=out_shape,
        compiler_params=pltpu.CompilerParams(dimension_semantics=("arbitrary",), vmem_limit_bytes=60 * 1024 * 1024),
        cost_estimate=pl.CostEstimate(flops=10_000_000_000, bytes_accessed=6_000_000, transcendentals=4_000_000),
        name="attention_first" if part == 0 else "attention_second",
    )(scal, rows_in, rows_in, doc_rows, *kv, *sums)


def by_head(rows):
    tokens = rows.shape[0]
    split = rows.reshape(tokens, 8, -1, HEAD_SIZE).transpose(1, 0, 2, 3)
    return split.reshape(8, -1, HEAD_SIZE)


def exchanged(block):
    return lax.all_to_all(block, "head", split_axis=0, concat_axis=0, tiled=True)


def plan(doc_lengths, stored_block_order):
    cell = lax.axis_index("ctx")
    starts = jnp.cumsum(doc_lengths) - doc_lengths
    window_first = (cell - (SLOTS - 1)) * CELL_BLOCKS
    padded = jnp.pad(stored_block_order, (WINDOW_BLOCKS - CELL_BLOCKS, 0))
    window_order = lax.dynamic_slice_in_dim(padded, cell * CELL_BLOCKS, WINDOW_BLOCKS, 0)
    base = jnp.arange(WINDOW_BLOCKS, dtype=jnp.int32) // CELL_BLOCKS * CELL_BLOCKS
    place = base + window_order % CELL_BLOCKS
    own_place = place[WINDOW_BLOCKS - CELL_BLOCKS :]
    own_block = window_first + own_place
    lane = lax.broadcasted_iota(jnp.int32, (PARTS, CELL_BLOCKS, 1, ROWS), 3)
    part = lax.broadcasted_iota(jnp.int32, (PARTS, CELL_BLOCKS, 1, ROWS), 0)
    token = lane // PART_ROWS * 64 + part * PART_TOKENS + lane % PART_ROWS // SHARE
    pos = own_block[None, :, None, None] * BLOCK + token
    begun = starts <= pos[..., None]
    doc_start = jnp.max(jnp.where(begun, starts, 0), axis=-1)
    doc_rows = (doc_start - window_first * BLOCK).astype(jnp.int32)
    edges = jnp.concatenate([own_block * BLOCK, own_block * BLOCK + BLOCK - 1])
    low = jnp.max(jnp.where(starts <= edges[:, None], starts, 0), axis=-1) - window_first * BLOCK
    scal = jnp.concatenate([place, own_place, low[:CELL_BLOCKS] // BLOCK, low[CELL_BLOCKS:]]).astype(jnp.int32)
    return scal, doc_rows


def body(queries, keys, values, out_grad, doc_lengths, stored_block_order):
    scal, doc_rows = plan(doc_lengths, stored_block_order)
    half = PART_TOKENS
    first_in = exchanged(
        jnp.concatenate([by_head(queries[:half]), by_head(out_grad[:half]), by_head(keys), by_head(values)], axis=1)
    )
    kv0 = first_in[:, 2 * PART_ROWS :, :]
    kv = (kv0, passed_along(kv0, "ctx", 1), passed_along(kv0, "ctx", 2))
    second_rows = jnp.concatenate([by_head(queries[half:]), by_head(out_grad[half:])], axis=1)
    second_rows, *kv = lax.optimization_barrier((second_rows, *kv))
    second_in = exchanged(second_rows)
    first_out, *sums = attention(0, scal, first_in, doc_rows[0], kv)
    first_back = exchanged(first_out)
    second_out, dkv0, dkv1, dkv2 = attention(1, scal, second_in, doc_rows[1], kv, sums)
    first_back, dkv1, dkv2 = lax.optimization_barrier((first_back, dkv1, dkv2))
    near, far = passed_along(dkv1, "ctx", -1), passed_along(dkv2, "ctx", -2)
    summed = dkv0.astype(jnp.float32) + near.astype(jnp.float32) + far.astype(jnp.float32)
    second_out = lax.dynamic_update_slice(second_out, summed.astype(jnp.bfloat16), (0, 2 * PART_ROWS, 0))
    second_back = exchanged(second_out)

    def by_token(block, tokens, heads):
        return block.reshape(8, tokens, heads, HEAD_SIZE).transpose(1, 0, 2, 3).reshape(tokens, -1, HEAD_SIZE)

    def joined(start):
        rows = slice(start, start + PART_ROWS)
        return jnp.concatenate([by_token(back[:, rows], half, SHARE) for back in (first_back, second_back)], axis=0)

    attended, query_grad = joined(0), joined(PART_ROWS)
    key_gradient = by_token(second_back[:, 2 * PART_ROWS : 2 * PART_ROWS + 64], 64, 1)
    value_gradient = by_token(second_back[:, 2 * PART_ROWS + 64 :], 64, 1)
    return attended, query_grad, key_gradient, value_gradient


def solution(mesh):
    spec = P(("ctx", "head"), None, None)
    return jax.shard_map(
        body,
        mesh=mesh,
        in_specs=(spec, spec, spec, spec, P(), P()),
        out_specs=(spec, spec, spec, spec),
        check_vma=False,
    )
```

```python
import functools
import math

import jax
import jax.numpy as jnp
from jax import lax
from jax.experimental import pallas as pl
from jax.experimental.pallas import tpu as pltpu
from jax.sharding import PartitionSpec as P

HEAD_SIZE = 128
BLOCK = 128
CELL_BLOCKS = 4
SLOTS = 3
WINDOW_BLOCKS = SLOTS * CELL_BLOCKS
WINDOW = WINDOW_BLOCKS * BLOCK
CHUNK = 2 * BLOCK
PADDED = WINDOW + BLOCK
REACH = 10 * BLOCK
SHARE = 8
ROWS = BLOCK * SHARE
TILE = ROWS // 2

SCALE = HEAD_SIZE ** (-0.5)
EXP2_SCALE = SCALE * math.log2(math.e)
NEG_BIG = -1e30

NT = (((1,), (1,)), ((), ()))
NN = (((1,), (0,)), ((), ()))
TN = (((0,), (0,)), ((), ()))


def dot(a, b, dims=NN):
    return lax.dot_general(a, b, dims, preferred_element_type=jnp.float32)


def passed_along(block, axis, distance):
    devices = range(lax.axis_size(axis))
    route = [(i - distance, i) for i in devices if i - distance in devices]
    return lax.ppermute(block, axis, route)


def stored_rows(kv_ref, block, which):
    first = kv_ref[2 * block, pl.ds(64 * which, 64), :]
    second = kv_ref[2 * block + 1, pl.ds(64 * which, 64), :]
    return jnp.concatenate([first, second], axis=0)


def window_start(scal_ref, slot, block):
    index = (SLOTS - 1 - slot) * CELL_BLOCKS + block
    return pl.multiple_of(scal_ref[index] * BLOCK, BLOCK)


def allowed_tile(key_start, first_block, doc_start, tile):
    lane = lax.broadcasted_iota(jnp.int32, (1, TILE), 1) + tile * TILE
    query_pos = first_block * BLOCK + lax.shift_right_logical(lane, 3)
    key_pos = lax.broadcasted_iota(jnp.int32, (CHUNK, TILE), 0)
    return (key_pos >= doc_start - key_start) & (key_pos <= query_pos - key_start)


def each_chunk(scal_ref, step, work):
    first_block = scal_ref[WINDOW_BLOCKS + step]
    low_block = scal_ref[WINDOW_BLOCKS + CELL_BLOCKS + step]
    last_start = scal_ref[WINDOW_BLOCKS + 2 * CELL_BLOCKS + step]
    chunks = lax.shift_right_logical(first_block - low_block + 2, 1)

    def turn_work(turn, _):
        key_start = pl.multiple_of((low_block + 2 * turn) * BLOCK, BLOCK)
        whole = (key_start >= last_start) & (key_start + CHUNK <= first_block * BLOCK)

        @pl.when(whole)
        def _():
            work(turn, key_start, first_block, False)

        @pl.when(jnp.logical_not(whole))
        def _():
            work(turn, key_start, first_block, True)

        return 0

    lax.fori_loop(0, chunks, turn_work, 0)


def forward_kernel(scal_ref, q_ref, doc_ref, kv0_ref, kv1_ref, kv2_ref, out_ref, out_t_ref, lse_ref, key_seq, value_t, scores, acc, top):
    step = pl.program_id(0)

    @pl.when(step == 0)
    def _():
        for slot, kv_ref in enumerate((kv0_ref, kv1_ref, kv2_ref)):
            for block in range(CELL_BLOCKS):
                start = window_start(scal_ref, slot, block)
                key_seq[pl.ds(start, BLOCK), :] = stored_rows(kv_ref, block, 0)
                value = stored_rows(kv_ref, block, 1).astype(jnp.float32)
                value_t[:, pl.ds(start, BLOCK)] = value.T.astype(jnp.bfloat16)
        key_seq[pl.ds(WINDOW, BLOCK), :] = jnp.zeros((BLOCK, HEAD_SIZE), jnp.bfloat16)
        value_t[:, pl.ds(WINDOW, BLOCK)] = jnp.zeros((HEAD_SIZE, BLOCK), jnp.bfloat16)

    top[...] = jnp.full_like(top, NEG_BIG)
    acc[...] = jnp.zeros_like(acc)

    def score_chunk(turn, key_start, first_block, masked):
        keys = key_seq[pl.ds(key_start, CHUNK), :]
        rows = pl.ds(pl.multiple_of(turn * CHUNK, CHUNK), CHUNK)
        for tile in range(2):
            cols = slice(tile * TILE, (tile + 1) * TILE)
            raw = dot(keys, q_ref[tile], NT)
            if masked:
                raw = jnp.where(allowed_tile(key_start, first_block, doc_ref[0, :, cols], tile), raw, NEG_BIG)
            scores[rows, cols] = raw
            part = jnp.max(raw.reshape(CHUNK // 8, 8, TILE), axis=0)
            top[:, cols] = jnp.maximum(top[:, cols], part)

    each_chunk(scal_ref, step, score_chunk)
    highest = jnp.max(top[...], axis=0, keepdims=True) * EXP2_SCALE
    top[...] = jnp.zeros_like(top)
    first_block = scal_ref[WINDOW_BLOCKS + step]
    low_block = scal_ref[WINDOW_BLOCKS + CELL_BLOCKS + step]

    def value_chunk(turn, _):
        key_start = pl.multiple_of((low_block + 2 * turn) * BLOCK, BLOCK)
        rows = pl.ds(pl.multiple_of(turn * CHUNK, CHUNK), CHUNK)
        values = value_t[:, pl.ds(key_start, CHUNK)]
        for tile in range(2):
            cols = slice(tile * TILE, (tile + 1) * TILE)
            weights = jnp.exp2(scores[rows, cols] * EXP2_SCALE - highest[:, cols])
            top[:, cols] += jnp.sum(weights.reshape(CHUNK // 8, 8, TILE), axis=0)
            acc[:, cols] += dot(values, weights.astype(jnp.bfloat16))
        return 0

    lax.fori_loop(0, lax.shift_right_logical(first_block - low_block + 2, 1), value_chunk, 0)
    total = jnp.sum(top[...], axis=0, keepdims=True)
    lse_ref[0] = highest + jnp.log2(total)
    out_t = acc[...] * (1.0 / total)
    out_t_ref[0] = out_t.astype(jnp.bfloat16)
    out = out_t.T.astype(jnp.bfloat16)
    out_ref[0] = out[: ROWS // 2]
    out_ref[1] = out[ROWS // 2 :]


def backward_kernel(scal_ref, q_ref, grad_ref, out_t_ref, lse_ref, doc_ref, kv0_ref, kv1_ref, kv2_ref, dq_ref, dkv0_ref, dkv1_ref, dkv2_ref, key_seq, value_seq, dk_acc, dv_acc, dq_acc, weights_low, grads_low, delta):
    step = pl.program_id(0)

    @pl.when(step == 0)
    def _():
        for slot, kv_ref in enumerate((kv0_ref, kv1_ref, kv2_ref)):
            for block in range(CELL_BLOCKS):
                start = window_start(scal_ref, slot, block)
                key_seq[pl.ds(start, BLOCK), :] = stored_rows(kv_ref, block, 0)
                value_seq[pl.ds(start, BLOCK), :] = stored_rows(kv_ref, block, 1)
        zeros = jnp.zeros((BLOCK, HEAD_SIZE), jnp.bfloat16)
        key_seq[pl.ds(WINDOW, BLOCK), :] = zeros
        value_seq[pl.ds(WINDOW, BLOCK), :] = zeros
        dk_acc[...] = jnp.zeros_like(dk_acc)
        dv_acc[...] = jnp.zeros_like(dv_acc)

    dq_acc[...] = jnp.zeros_like(dq_acc)
    for half in range(2):
        cols = slice(half * TILE, (half + 1) * TILE)
        grad_t = grad_ref[half].astype(jnp.float32).T
        delta[:, cols] = jnp.sum(grad_t * out_t_ref[0, :, cols].astype(jnp.float32), axis=0, keepdims=True)

    def chunk(turn, key_start, first_block, masked):
        keys = key_seq[pl.ds(key_start, CHUNK), :]
        values = value_seq[pl.ds(key_start, CHUNK), :]
        for tile in range(2):
            cols = slice(tile * TILE, (tile + 1) * TILE)
            raw = dot(keys, q_ref[tile], NT)
            scaled = raw * EXP2_SCALE - lse_ref[0, :, cols]
            if masked:
                scaled = jnp.where(allowed_tile(key_start, first_block, doc_ref[0, :, cols], tile), scaled, NEG_BIG)
            weights = jnp.exp2(scaled)
            weights_low[:, cols] = weights.astype(jnp.bfloat16)
            sent = dot(values, grad_ref[tile], NT)
            grads_low[:, cols] = (weights * (sent - delta[:, cols])).astype(jnp.bfloat16)
        queries = jnp.concatenate([q_ref[0], q_ref[1]], axis=0)
        out_grads = jnp.concatenate([grad_ref[0], grad_ref[1]], axis=0)
        dq_acc[...] += dot(grads_low[...], keys, TN)
        dk_acc[pl.ds(key_start, CHUNK), :] += dot(grads_low[...], queries)
        dv_acc[pl.ds(key_start, CHUNK), :] += dot(weights_low[...], out_grads)

    each_chunk(scal_ref, step, chunk)
    query_grad = (dq_acc[...] * SCALE).astype(jnp.bfloat16)
    dq_ref[0] = query_grad[:TILE]
    dq_ref[1] = query_grad[TILE:]

    @pl.when(step == CELL_BLOCKS - 1)
    def _():
        for slot, dkv_ref in enumerate((dkv0_ref, dkv1_ref, dkv2_ref)):
            for block in range(CELL_BLOCKS):
                start = window_start(scal_ref, slot, block)
                dk = (dk_acc[pl.ds(start, BLOCK), :] * SCALE).astype(jnp.bfloat16)
                dv = dv_acc[pl.ds(start, BLOCK), :].astype(jnp.bfloat16)
                for half in range(2):
                    rows = slice(half * 64, (half + 1) * 64)
                    dkv_ref[2 * block + half, pl.ds(0, 64), :] = dk[rows]
                    dkv_ref[2 * block + half, pl.ds(64, 64), :] = dv[rows]


def row_spec():
    return pl.BlockSpec((2, ROWS // 2, HEAD_SIZE), lambda b, s: (b, 0, 0))


def lane_spec(rows):
    return pl.BlockSpec((1, rows, ROWS), lambda b, s: (b, 0, 0))


def kv_spec():
    return pl.BlockSpec((8, 128, HEAD_SIZE), lambda b, s: (0, 0, 0))


def params(mebibytes):
    return pltpu.CompilerParams(dimension_semantics=("arbitrary",), vmem_limit_bytes=mebibytes * 1024 * 1024)


def forward(scal, q_in, doc_rows, kv):
    return pl.pallas_call(
        forward_kernel,
        grid_spec=pltpu.PrefetchScalarGridSpec(
            num_scalar_prefetch=1,
            grid=(CELL_BLOCKS,),
            in_specs=[row_spec(), lane_spec(1), kv_spec(), kv_spec(), kv_spec()],
            out_specs=[row_spec(), lane_spec(HEAD_SIZE), lane_spec(1)],
            scratch_shapes=[
                pltpu.VMEM((PADDED, HEAD_SIZE), jnp.bfloat16),
                pltpu.VMEM((HEAD_SIZE, PADDED), jnp.bfloat16),
                pltpu.VMEM((REACH, ROWS), jnp.float32),
                pltpu.VMEM((HEAD_SIZE, ROWS), jnp.float32),
                pltpu.VMEM((8, ROWS), jnp.float32),
            ],
        ),
        out_shape=[
            jax.ShapeDtypeStruct((8, ROWS // 2, HEAD_SIZE), jnp.bfloat16),
            jax.ShapeDtypeStruct((CELL_BLOCKS, HEAD_SIZE, ROWS), jnp.bfloat16),
            jax.ShapeDtypeStruct((CELL_BLOCKS, 1, ROWS), jnp.float32),
        ],
        compiler_params=params(60),
        cost_estimate=pl.CostEstimate(flops=4_000_000_000, bytes_accessed=4_000_000, transcendentals=4_000_000),
        name="forward",
    )(scal, q_in, doc_rows, *kv)


def backward(scal, q_in, grad_in, out_t, lse, doc_rows, kv):
    dkv_shape = jax.ShapeDtypeStruct((8, 128, HEAD_SIZE), jnp.bfloat16)
    return pl.pallas_call(
        backward_kernel,
        grid_spec=pltpu.PrefetchScalarGridSpec(
            num_scalar_prefetch=1,
            grid=(CELL_BLOCKS,),
            in_specs=[row_spec(), row_spec(), lane_spec(HEAD_SIZE), lane_spec(1), lane_spec(1), kv_spec(), kv_spec(), kv_spec()],
            out_specs=[row_spec(), kv_spec(), kv_spec(), kv_spec()],
            scratch_shapes=[
                pltpu.VMEM((PADDED, HEAD_SIZE), jnp.bfloat16),
                pltpu.VMEM((PADDED, HEAD_SIZE), jnp.bfloat16),
                pltpu.VMEM((PADDED, HEAD_SIZE), jnp.float32),
                pltpu.VMEM((PADDED, HEAD_SIZE), jnp.float32),
                pltpu.VMEM((ROWS, HEAD_SIZE), jnp.float32),
                pltpu.VMEM((CHUNK, ROWS), jnp.bfloat16),
                pltpu.VMEM((CHUNK, ROWS), jnp.bfloat16),
                pltpu.VMEM((1, ROWS), jnp.float32),
            ],
        ),
        out_shape=[jax.ShapeDtypeStruct((8, ROWS // 2 + 128, HEAD_SIZE), jnp.bfloat16), dkv_shape, dkv_shape, dkv_shape],
        compiler_params=params(59),
        cost_estimate=pl.CostEstimate(flops=10_000_000_000, bytes_accessed=6_000_000, transcendentals=4_000_000),
        name="backward",
    )(scal, q_in, grad_in, out_t, lse, doc_rows, *kv)


def by_head(rows):
    tokens = rows.shape[0]
    split = rows.reshape(tokens, 8, -1, HEAD_SIZE).transpose(1, 0, 2, 3)
    return split.reshape(8, -1, HEAD_SIZE)


def exchanged(block):
    return lax.all_to_all(block, "head", split_axis=0, concat_axis=0, tiled=True)


def plan(doc_lengths, stored_block_order):
    cell = lax.axis_index("ctx")
    starts = jnp.cumsum(doc_lengths) - doc_lengths
    window_first = (cell - (SLOTS - 1)) * CELL_BLOCKS
    padded = jnp.pad(stored_block_order, (WINDOW_BLOCKS - CELL_BLOCKS, 0))
    window_order = lax.dynamic_slice_in_dim(padded, cell * CELL_BLOCKS, WINDOW_BLOCKS, 0)
    base = jnp.arange(WINDOW_BLOCKS, dtype=jnp.int32) // CELL_BLOCKS * CELL_BLOCKS
    place = base + window_order % CELL_BLOCKS
    own_place = place[WINDOW_BLOCKS - CELL_BLOCKS :]
    own_block = window_first + own_place
    token = lax.broadcasted_iota(jnp.int32, (CELL_BLOCKS, 1, ROWS), 2) // SHARE
    pos = own_block[:, None, None] * BLOCK + token
    begun = starts <= pos[..., None]
    doc_start = jnp.max(jnp.where(begun, starts, 0), axis=-1)
    doc_rows = doc_start - window_first * BLOCK
    edges = jnp.concatenate([own_block * BLOCK, own_block * BLOCK + BLOCK - 1])
    low = jnp.max(jnp.where(starts <= edges[:, None], starts, 0), axis=-1) - window_first * BLOCK
    scal = jnp.concatenate([place, own_place, low[:CELL_BLOCKS] // BLOCK, low[CELL_BLOCKS:]]).astype(jnp.int32)
    return scal, doc_rows.astype(jnp.int32)


def body(queries, keys, values, out_grad, doc_lengths, stored_block_order):
    scal, doc_rows = plan(doc_lengths, stored_block_order)
    first_in = exchanged(jnp.concatenate([by_head(queries), by_head(keys), by_head(values)], axis=1))
    kv0 = first_in[:, 512:, :]
    kv = (kv0, passed_along(kv0, "ctx", 1), passed_along(kv0, "ctx", 2))
    grad_rows, *kv = lax.optimization_barrier((by_head(out_grad), *kv))
    grad_in = exchanged(grad_rows)
    attended_loc, out_t, lse = forward(scal, first_in, doc_rows, kv)
    attended_in = exchanged(attended_loc)
    last_loc, dkv0, dkv1, dkv2 = backward(scal, first_in, grad_in, out_t, lse, doc_rows, kv)
    attended_in, dkv1, dkv2 = lax.optimization_barrier((attended_in, dkv1, dkv2))
    near, far = passed_along(dkv1, "ctx", -1), passed_along(dkv2, "ctx", -2)
    summed = dkv0.astype(jnp.float32) + near.astype(jnp.float32) + far.astype(jnp.float32)
    last_loc = lax.dynamic_update_slice(last_loc, summed.astype(jnp.bfloat16), (0, 512, 0))
    last_in = exchanged(last_loc)
    tokens = queries.shape[0]

    def by_token(block, heads):
        return block.reshape(8, tokens, heads, HEAD_SIZE).transpose(1, 0, 2, 3).reshape(tokens, -1, HEAD_SIZE)

    attended = by_token(attended_in, SHARE)
    query_grad = by_token(last_in[:, :512], SHARE)
    key_gradient = by_token(last_in[:, 512:576], 1)
    value_gradient = by_token(last_in[:, 576:], 1)
    return attended, query_grad, key_gradient, value_gradient


def solution(mesh):
    spec = P(("ctx", "head"), None, None)
    return jax.shard_map(
        body,
        mesh=mesh,
        in_specs=(spec, spec, spec, spec, P(), P()),
        out_specs=(spec, spec, spec, spec),
        check_vma=False,
    )
```

```python
import functools
import math

import jax
import jax.numpy as jnp
from jax import lax
from jax.experimental import pallas as pl
from jax.experimental.pallas import tpu as pltpu
from jax.sharding import PartitionSpec as P

HEAD_SIZE = 128
BLOCK = 128
CELL_BLOCKS = 4
SLOTS = 3
WINDOW_BLOCKS = SLOTS * CELL_BLOCKS
WINDOW = WINDOW_BLOCKS * BLOCK
CHUNK = 2 * BLOCK
PADDED = WINDOW + BLOCK
REACH = 10 * BLOCK
SHARE = 8
HALF = 64 * SHARE
ROWS = 2 * HALF

SCALE = HEAD_SIZE ** (-0.5)
EXP2_SCALE = SCALE * math.log2(math.e)
NEG_BIG = -1e30

NT = (((1,), (1,)), ((), ()))
NN = (((1,), (0,)), ((), ()))
TN = (((0,), (0,)), ((), ()))


def dot(a, b, dims=NN):
    return lax.dot_general(a, b, dims, preferred_element_type=jnp.float32)


def passed_along(block, axis, distance):
    devices = range(lax.axis_size(axis))
    route = [(i - distance, i) for i in devices if i - distance in devices]
    return lax.ppermute(block, axis, route)


def stored_rows(kv_ref, block, which):
    first = kv_ref[2 * block, pl.ds(64 * which, 64), :]
    second = kv_ref[2 * block + 1, pl.ds(64 * which, 64), :]
    return jnp.concatenate([first, second], axis=0)


def window_start(scal_ref, slot, block):
    index = (SLOTS - 1 - slot) * CELL_BLOCKS + block
    return pl.multiple_of(scal_ref[index] * BLOCK, BLOCK)


def allowed_tile(key_start, count, first_block, doc_start, tile):
    lane = lax.broadcasted_iota(jnp.int32, (1, HALF), 1) + tile * HALF
    query_pos = first_block * BLOCK + lax.shift_right_logical(lane, 3)
    key_pos = lax.broadcasted_iota(jnp.int32, (count, HALF), 0)
    return (key_pos >= doc_start - key_start) & (key_pos <= query_pos - key_start)


def attention_kernel(scal_ref, q_ref, grad_ref, doc_ref, kv0_ref, kv1_ref, kv2_ref, out_ref, dkv0_ref, dkv1_ref, dkv2_ref, key_seq, value_seq, value_t, scores, acc, top, dq_acc, dk_acc, dv_acc, weights_low, grads_low):
    step = pl.program_id(0)

    @pl.when(step == 0)
    def _():
        for slot, kv_ref in enumerate((kv0_ref, kv1_ref, kv2_ref)):
            for block in range(CELL_BLOCKS):
                start = window_start(scal_ref, slot, block)
                key_seq[pl.ds(start, BLOCK), :] = stored_rows(kv_ref, block, 0)
                value = stored_rows(kv_ref, block, 1)
                value_seq[pl.ds(start, BLOCK), :] = value
                value_t[:, pl.ds(start, BLOCK)] = value.astype(jnp.float32).T.astype(jnp.bfloat16)
        zeros = jnp.zeros((BLOCK, HEAD_SIZE), jnp.bfloat16)
        key_seq[pl.ds(WINDOW, BLOCK), :] = zeros
        value_seq[pl.ds(WINDOW, BLOCK), :] = zeros
        value_t[:, pl.ds(WINDOW, BLOCK)] = zeros
        dk_acc[...] = jnp.zeros_like(dk_acc)
        dv_acc[...] = jnp.zeros_like(dv_acc)

    first_block = scal_ref[WINDOW_BLOCKS + step]
    low_block = scal_ref[WINDOW_BLOCKS + CELL_BLOCKS + step]
    last_start = scal_ref[WINDOW_BLOCKS + 2 * CELL_BLOCKS + step]
    chunks = lax.shift_right_logical(first_block - low_block + 2, 1)
    pairs = lax.shift_right_logical(chunks, 1)
    top[...] = jnp.full_like(top, NEG_BIG)
    acc[...] = jnp.zeros_like(acc)
    dq_acc[...] = jnp.zeros_like(dq_acc)

    def span(turn, count):
        key_start = pl.multiple_of((low_block + 4 * turn) * BLOCK, BLOCK)
        return key_start, pl.ds(key_start, count), pl.ds(pl.multiple_of(turn * 2 * CHUNK, CHUNK), count)

    def score(turn, count, masked):
        key_start, window, rows = span(turn, count)
        for tile in range(2):
            cols = slice(tile * HALF, (tile + 1) * HALF)
            raw = dot(key_seq[window, :], q_ref[tile], NT)
            if masked:
                allowed = allowed_tile(key_start, count, first_block, doc_ref[0, :, cols], tile)
                raw = jnp.where(allowed, raw, NEG_BIG)
            scores[rows, cols] = raw
            top[:, cols] = jnp.maximum(top[:, cols], jnp.max(raw.reshape(count // 8, 8, HALF), axis=0))

    def score_pair(turn, _):
        key_start = (low_block + 4 * turn) * BLOCK
        whole = (key_start >= last_start) & (key_start + 2 * CHUNK <= first_block * BLOCK)
        pl.when(whole)(lambda: score(turn, 2 * CHUNK, False))
        pl.when(jnp.logical_not(whole))(lambda: score(turn, 2 * CHUNK, True))
        return 0

    lax.fori_loop(0, pairs, score_pair, 0)
    pl.when(chunks > 2 * pairs)(lambda: score(pairs, CHUNK, True))
    highest = jnp.max(top[...], axis=0, keepdims=True) * EXP2_SCALE
    top[...] = jnp.zeros_like(top)

    def weigh(turn, count):
        _, window, rows = span(turn, count)
        for tile in range(2):
            cols = slice(tile * HALF, (tile + 1) * HALF)
            weights = jnp.exp2(scores[rows, cols] * EXP2_SCALE - highest[:, cols])
            top[:, cols] += jnp.sum(weights.reshape(count // 8, 8, HALF), axis=0)
            acc[:, cols] += dot(value_t[:, window], weights.astype(jnp.bfloat16))

    def weigh_pair(turn, _):
        weigh(turn, 2 * CHUNK)
        return 0

    lax.fori_loop(0, pairs, weigh_pair, 0)
    pl.when(chunks > 2 * pairs)(lambda: weigh(pairs, CHUNK))
    total = jnp.sum(top[...], axis=0, keepdims=True)
    lse = highest + jnp.log2(total)
    out = (acc[...] * (1.0 / total)).T.astype(jnp.bfloat16)
    out_ref[:, :HALF, :] = out.reshape(2, HALF, HEAD_SIZE)
    delta = jnp.sum((out.astype(jnp.float32) * grad_ref[...].reshape(ROWS, HEAD_SIZE).astype(jnp.float32)).T, axis=0, keepdims=True)

    def grad_chunk(turn, _):
        window = pl.ds(pl.multiple_of((low_block + 2 * turn) * BLOCK, BLOCK), CHUNK)
        rows = pl.ds(pl.multiple_of(turn * CHUNK, CHUNK), CHUNK)
        keys = key_seq[window, :]
        for tile in range(2):
            cols = slice(tile * HALF, (tile + 1) * HALF)
            weights = jnp.exp2(scores[rows, cols] * EXP2_SCALE - lse[:, cols])
            weights_low[:, cols] = weights.astype(jnp.bfloat16)
            sent = dot(value_seq[window, :], grad_ref[tile], NT)
            grads_low[:, cols] = (weights * (sent - delta[:, cols])).astype(jnp.bfloat16)
        dq_acc[...] += dot(grads_low[...], keys, TN)
        dk_acc[window, :] += dot(grads_low[...], q_ref[...].reshape(ROWS, HEAD_SIZE))
        dv_acc[window, :] += dot(weights_low[...], grad_ref[...].reshape(ROWS, HEAD_SIZE))
        return 0

    lax.fori_loop(0, chunks, grad_chunk, 0)
    query_grad = (dq_acc[...] * SCALE).astype(jnp.bfloat16)
    out_ref[:, HALF:, :] = query_grad.reshape(2, HALF, HEAD_SIZE)

    @pl.when(step == CELL_BLOCKS - 1)
    def _():
        for slot, dkv_ref in enumerate((dkv0_ref, dkv1_ref, dkv2_ref)):
            for block in range(CELL_BLOCKS):
                start = window_start(scal_ref, slot, block)
                dk = (dk_acc[pl.ds(start, BLOCK), :] * SCALE).astype(jnp.bfloat16)
                dv = dv_acc[pl.ds(start, BLOCK), :].astype(jnp.bfloat16)
                for half in range(2):
                    rows = slice(half * 64, (half + 1) * 64)
                    dkv_ref[2 * block + half, pl.ds(0, 64), :] = dk[rows]
                    dkv_ref[2 * block + half, pl.ds(64, 64), :] = dv[rows]


def attention(scal, rows_in, doc_rows, kv):
    def row_spec(place):
        return pl.BlockSpec((2, HALF, HEAD_SIZE), lambda b, s: (b, place, 0))

    kv_spec = pl.BlockSpec((8, 128, HEAD_SIZE), lambda b, s: (0, 0, 0))
    return pl.pallas_call(
        attention_kernel,
        grid_spec=pltpu.PrefetchScalarGridSpec(
            num_scalar_prefetch=1,
            grid=(CELL_BLOCKS,),
            in_specs=[row_spec(0), row_spec(1), pl.BlockSpec((1, 1, ROWS), lambda b, s: (b, 0, 0))] + [kv_spec] * 3,
            out_specs=[pl.BlockSpec((2, 2 * HALF, HEAD_SIZE), lambda b, s: (b, 0, 0))] + [kv_spec] * 3,
            scratch_shapes=[
                pltpu.VMEM((PADDED, HEAD_SIZE), jnp.bfloat16),
                pltpu.VMEM((PADDED, HEAD_SIZE), jnp.bfloat16),
                pltpu.VMEM((HEAD_SIZE, PADDED), jnp.bfloat16),
                pltpu.VMEM((REACH, ROWS), jnp.float32),
                pltpu.VMEM((HEAD_SIZE, ROWS), jnp.float32),
                pltpu.VMEM((8, ROWS), jnp.float32),
                pltpu.VMEM((ROWS, HEAD_SIZE), jnp.float32),
                pltpu.VMEM((PADDED, HEAD_SIZE), jnp.float32),
                pltpu.VMEM((PADDED, HEAD_SIZE), jnp.float32),
                pltpu.VMEM((CHUNK, ROWS), jnp.bfloat16),
                pltpu.VMEM((CHUNK, ROWS), jnp.bfloat16),
            ],
        ),
        out_shape=[jax.ShapeDtypeStruct((8, 2 * HALF + 128, HEAD_SIZE), jnp.bfloat16)] + [jax.ShapeDtypeStruct((8, 128, HEAD_SIZE), jnp.bfloat16)] * 3,
        compiler_params=pltpu.CompilerParams(dimension_semantics=("arbitrary",), vmem_limit_bytes=60 * 1024 * 1024),
        cost_estimate=pl.CostEstimate(flops=10_000_000_000, bytes_accessed=6_000_000, transcendentals=4_000_000),
        name="attention",
    )(scal, rows_in, rows_in, doc_rows, *kv)


def by_head(rows):
    tokens = rows.shape[0]
    split = rows.reshape(tokens, 8, -1, HEAD_SIZE).transpose(1, 0, 2, 3)
    return split.reshape(8, -1, HEAD_SIZE)


def exchanged(block):
    return lax.all_to_all(block, "head", split_axis=0, concat_axis=0, tiled=True)


def plan(doc_lengths, stored_block_order):
    cell = lax.axis_index("ctx")
    starts = jnp.cumsum(doc_lengths) - doc_lengths
    window_first = (cell - (SLOTS - 1)) * CELL_BLOCKS
    padded = jnp.pad(stored_block_order, (WINDOW_BLOCKS - CELL_BLOCKS, 0))
    window_order = lax.dynamic_slice_in_dim(padded, cell * CELL_BLOCKS, WINDOW_BLOCKS, 0)
    base = jnp.arange(WINDOW_BLOCKS, dtype=jnp.int32) // CELL_BLOCKS * CELL_BLOCKS
    place = base + window_order % CELL_BLOCKS
    own_place = place[WINDOW_BLOCKS - CELL_BLOCKS :]
    own_block = window_first + own_place
    token = lax.broadcasted_iota(jnp.int32, (CELL_BLOCKS, 1, ROWS), 2) // SHARE
    pos = own_block[:, None, None] * BLOCK + token
    begun = starts <= pos[..., None]
    doc_start = jnp.max(jnp.where(begun, starts, 0), axis=-1)
    doc_rows = (doc_start - window_first * BLOCK).astype(jnp.int32)
    edges = jnp.concatenate([own_block * BLOCK, own_block * BLOCK + BLOCK - 1])
    low = jnp.max(jnp.where(starts <= edges[:, None], starts, 0), axis=-1) - window_first * BLOCK
    scal = jnp.concatenate([place, own_place, low[:CELL_BLOCKS] // BLOCK, low[CELL_BLOCKS:]]).astype(jnp.int32)
    return scal, doc_rows


def body(queries, keys, values, out_grad, doc_lengths, stored_block_order):
    scal, doc_rows = plan(doc_lengths, stored_block_order)
    first_in = exchanged(jnp.concatenate([by_head(queries), by_head(out_grad), by_head(keys), by_head(values)], axis=1))
    kv0 = first_in[:, 2 * HALF :, :]
    kv = (kv0, passed_along(kv0, "ctx", 1), passed_along(kv0, "ctx", 2))
    rows_out, dkv0, dkv1, dkv2 = attention(scal, first_in, doc_rows, kv)
    near, far = passed_along(dkv1, "ctx", -1), passed_along(dkv2, "ctx", -2)
    summed = dkv0.astype(jnp.float32) + near.astype(jnp.float32) + far.astype(jnp.float32)
    rows_out = lax.dynamic_update_slice(rows_out, summed.astype(jnp.bfloat16), (0, 2 * HALF, 0))
    back = exchanged(rows_out)
    tokens = queries.shape[0]

    def by_token(block, heads):
        return block.reshape(8, tokens, heads, HEAD_SIZE).transpose(1, 0, 2, 3).reshape(tokens, -1, HEAD_SIZE)

    attended, query_grad = by_token(back[:, :HALF], SHARE), by_token(back[:, HALF : 2 * HALF], SHARE)
    key_gradient = by_token(back[:, 2 * HALF : 2 * HALF + 64], 1)
    value_gradient = by_token(back[:, 2 * HALF + 64 :], 1)
    return attended, query_grad, key_gradient, value_gradient


def solution(mesh):
    spec = P(("ctx", "head"), None, None)
    return jax.shard_map(
        body,
        mesh=mesh,
        in_specs=(spec, spec, spec, spec, P(), P()),
        out_specs=(spec, spec, spec, spec),
        check_vma=False,
    )
```

```python
import functools
import math

import jax
import jax.numpy as jnp
from jax import lax
from jax.experimental import pallas as pl
from jax.experimental.pallas import tpu as pltpu
from jax.sharding import PartitionSpec as P

HEAD_SIZE = 128
BLOCK = 128
CELL_BLOCKS = 4
SLOTS = 3
WINDOW_BLOCKS = SLOTS * CELL_BLOCKS
WINDOW = WINDOW_BLOCKS * BLOCK
CHUNK = 2 * BLOCK
PADDED = WINDOW + BLOCK
REACH = 10 * BLOCK
SHARE = 8
HALF = 64 * SHARE
ROWS = 2 * HALF

SCALE = HEAD_SIZE ** (-0.5)
EXP2_SCALE = SCALE * math.log2(math.e)
NEG_BIG = -1e30

NT = (((1,), (1,)), ((), ()))
NN = (((1,), (0,)), ((), ()))
TN = (((0,), (0,)), ((), ()))


def dot(a, b, dims=NN):
    return lax.dot_general(a, b, dims, preferred_element_type=jnp.float32)


def passed_along(block, axis, distance):
    devices = range(lax.axis_size(axis))
    route = [(i - distance, i) for i in devices if i - distance in devices]
    return lax.ppermute(block, axis, route)


def stored_rows(kv_ref, block, which):
    first = kv_ref[2 * block, pl.ds(64 * which, 64), :]
    second = kv_ref[2 * block + 1, pl.ds(64 * which, 64), :]
    return jnp.concatenate([first, second], axis=0)


def window_start(scal_ref, slot, block):
    index = (SLOTS - 1 - slot) * CELL_BLOCKS + block
    return pl.multiple_of(scal_ref[index] * BLOCK, BLOCK)


def allowed_tile(key_start, count, first_block, doc_start, tile):
    lane = lax.broadcasted_iota(jnp.int32, (1, HALF), 1) + tile * HALF
    query_pos = first_block * BLOCK + lax.shift_right_logical(lane, 3)
    key_pos = lax.broadcasted_iota(jnp.int32, (count, HALF), 0)
    return (key_pos >= doc_start - key_start) & (key_pos <= query_pos - key_start)


def attention_kernel(scal_ref, q_ref, grad_ref, doc_ref, kv0_ref, kv1_ref, kv2_ref, out_ref, dkv0_ref, dkv1_ref, dkv2_ref, key_seq, value_seq, value_t, scores, acc, top, dq_acc, dk_acc, dv_acc, weights_low, grads_low):
    step = pl.program_id(0)

    @pl.when(step == 0)
    def _():
        for slot, kv_ref in enumerate((kv0_ref, kv1_ref, kv2_ref)):
            for block in range(CELL_BLOCKS):
                start = window_start(scal_ref, slot, block)
                key_seq[pl.ds(start, BLOCK), :] = stored_rows(kv_ref, block, 0)
                value = stored_rows(kv_ref, block, 1)
                value_seq[pl.ds(start, BLOCK), :] = value
                value_t[:, pl.ds(start, BLOCK)] = value.astype(jnp.float32).T.astype(jnp.bfloat16)
        zeros = jnp.zeros((BLOCK, HEAD_SIZE), jnp.bfloat16)
        key_seq[pl.ds(WINDOW, BLOCK), :] = zeros
        value_seq[pl.ds(WINDOW, BLOCK), :] = zeros
        value_t[:, pl.ds(WINDOW, BLOCK)] = zeros
        dk_acc[...] = jnp.zeros_like(dk_acc)
        dv_acc[...] = jnp.zeros_like(dv_acc)

    first_block = scal_ref[WINDOW_BLOCKS + step]
    low_block = scal_ref[WINDOW_BLOCKS + CELL_BLOCKS + step]
    last_start = scal_ref[WINDOW_BLOCKS + 2 * CELL_BLOCKS + step]
    chunks = lax.shift_right_logical(first_block - low_block + 2, 1)
    pairs = lax.shift_right_logical(chunks, 1)
    top[...] = jnp.full_like(top, NEG_BIG)
    acc[...] = jnp.zeros_like(acc)
    dq_acc[...] = jnp.zeros_like(dq_acc)

    def span(turn, count):
        key_start = pl.multiple_of((low_block + 4 * turn) * BLOCK, BLOCK)
        return key_start, pl.ds(key_start, count), pl.ds(pl.multiple_of(turn * 2 * CHUNK, CHUNK), count)

    def score(turn, count, masked):
        key_start, window, rows = span(turn, count)
        for tile in range(2):
            cols = slice(tile * HALF, (tile + 1) * HALF)
            raw = dot(key_seq[window, :], q_ref[tile], NT)
            if masked:
                allowed = allowed_tile(key_start, count, first_block, doc_ref[0, :, cols], tile)
                raw = jnp.where(allowed, raw, NEG_BIG)
            scores[rows, cols] = raw
            top[:, cols] = jnp.maximum(top[:, cols], jnp.max(raw.reshape(count // 8, 8, HALF), axis=0))

    def score_pair(turn, _):
        key_start = (low_block + 4 * turn) * BLOCK
        whole = (key_start >= last_start) & (key_start + 2 * CHUNK <= first_block * BLOCK)
        pl.when(whole)(lambda: score(turn, 2 * CHUNK, False))
        pl.when(jnp.logical_not(whole))(lambda: score(turn, 2 * CHUNK, True))
        return 0

    lax.fori_loop(0, pairs, score_pair, 0)
    pl.when(chunks > 2 * pairs)(lambda: score(pairs, CHUNK, True))
    highest = jnp.max(top[...], axis=0, keepdims=True) * EXP2_SCALE
    top[...] = jnp.zeros_like(top)

    def weigh(turn, count):
        _, window, rows = span(turn, count)
        for tile in range(2):
            cols = slice(tile * HALF, (tile + 1) * HALF)
            weights = jnp.exp2(scores[rows, cols] * EXP2_SCALE - highest[:, cols])
            top[:, cols] += jnp.sum(weights.reshape(count // 8, 8, HALF), axis=0)
            acc[:, cols] += dot(value_t[:, window], weights.astype(jnp.bfloat16))

    def weigh_pair(turn, _):
        weigh(turn, 2 * CHUNK)
        return 0

    lax.fori_loop(0, pairs, weigh_pair, 0)
    pl.when(chunks > 2 * pairs)(lambda: weigh(pairs, CHUNK))
    total = jnp.sum(top[...], axis=0, keepdims=True)
    lse = highest + jnp.log2(total)
    out = (acc[...] * (1.0 / total)).T.astype(jnp.bfloat16)
    out_ref[:, :HALF, :] = out.reshape(2, HALF, HEAD_SIZE)
    delta = jnp.sum((out.astype(jnp.float32) * grad_ref[...].reshape(ROWS, HEAD_SIZE).astype(jnp.float32)).T, axis=0, keepdims=True)

    def grad_chunk(turn, _):
        window = pl.ds(pl.multiple_of((low_block + 2 * turn) * BLOCK, BLOCK), CHUNK)
        rows = pl.ds(pl.multiple_of(turn * CHUNK, CHUNK), CHUNK)
        keys = key_seq[window, :]
        for tile in range(2):
            cols = slice(tile * HALF, (tile + 1) * HALF)
            weights = jnp.exp2(scores[rows, cols] * EXP2_SCALE - lse[:, cols])
            weights_low[:, cols] = weights.astype(jnp.bfloat16)
            sent = dot(value_seq[window, :], grad_ref[tile], NT)
            grads_low[:, cols] = (weights * (sent - delta[:, cols])).astype(jnp.bfloat16)
        dq_acc[...] += dot(grads_low[...], keys, TN)
        dk_acc[window, :] += dot(grads_low[...], q_ref[...].reshape(ROWS, HEAD_SIZE))
        dv_acc[window, :] += dot(weights_low[...], grad_ref[...].reshape(ROWS, HEAD_SIZE))
        return 0

    lax.fori_loop(0, chunks, grad_chunk, 0)
    query_grad = (dq_acc[...] * SCALE).astype(jnp.bfloat16)
    out_ref[:, HALF:, :] = query_grad.reshape(2, HALF, HEAD_SIZE)

    @pl.when(step == CELL_BLOCKS - 1)
    def _():
        for slot, dkv_ref in enumerate((dkv0_ref, dkv1_ref, dkv2_ref)):
            for block in range(CELL_BLOCKS):
                start = window_start(scal_ref, slot, block)
                dk = (dk_acc[pl.ds(start, BLOCK), :] * SCALE).astype(jnp.bfloat16)
                dv = dv_acc[pl.ds(start, BLOCK), :].astype(jnp.bfloat16)
                for half in range(2):
                    rows = slice(half * 64, (half + 1) * 64)
                    dkv_ref[2 * block + half, pl.ds(0, 64), :] = dk[rows]
                    dkv_ref[2 * block + half, pl.ds(64, 64), :] = dv[rows]


def attention(scal, q_in, grad_in, doc_rows, kv):
    row_spec = pl.BlockSpec((2, HALF, HEAD_SIZE), lambda b, s: (b, 0, 0))
    kv_spec = pl.BlockSpec((8, 128, HEAD_SIZE), lambda b, s: (0, 0, 0))
    return pl.pallas_call(
        attention_kernel,
        grid_spec=pltpu.PrefetchScalarGridSpec(
            num_scalar_prefetch=1,
            grid=(CELL_BLOCKS,),
            in_specs=[row_spec, row_spec, pl.BlockSpec((1, 1, ROWS), lambda b, s: (b, 0, 0))] + [kv_spec] * 3,
            out_specs=[pl.BlockSpec((2, 2 * HALF, HEAD_SIZE), lambda b, s: (b, 0, 0))] + [kv_spec] * 3,
            scratch_shapes=[
                pltpu.VMEM((PADDED, HEAD_SIZE), jnp.bfloat16),
                pltpu.VMEM((PADDED, HEAD_SIZE), jnp.bfloat16),
                pltpu.VMEM((HEAD_SIZE, PADDED), jnp.bfloat16),
                pltpu.VMEM((REACH, ROWS), jnp.float32),
                pltpu.VMEM((HEAD_SIZE, ROWS), jnp.float32),
                pltpu.VMEM((8, ROWS), jnp.float32),
                pltpu.VMEM((ROWS, HEAD_SIZE), jnp.float32),
                pltpu.VMEM((PADDED, HEAD_SIZE), jnp.float32),
                pltpu.VMEM((PADDED, HEAD_SIZE), jnp.float32),
                pltpu.VMEM((CHUNK, ROWS), jnp.bfloat16),
                pltpu.VMEM((CHUNK, ROWS), jnp.bfloat16),
            ],
        ),
        out_shape=[jax.ShapeDtypeStruct((8, 2 * HALF, HEAD_SIZE), jnp.bfloat16)] + [jax.ShapeDtypeStruct((8, 128, HEAD_SIZE), jnp.bfloat16)] * 3,
        compiler_params=pltpu.CompilerParams(dimension_semantics=("arbitrary",), vmem_limit_bytes=60 * 1024 * 1024),
        cost_estimate=pl.CostEstimate(flops=10_000_000_000, bytes_accessed=6_000_000, transcendentals=4_000_000),
        name="attention",
    )(scal, q_in, grad_in, doc_rows, *kv)


def by_head(rows):
    tokens = rows.shape[0]
    split = rows.reshape(tokens, 8, -1, HEAD_SIZE).transpose(1, 0, 2, 3)
    return split.reshape(8, -1, HEAD_SIZE)


def exchanged(block):
    return lax.all_to_all(block, "head", split_axis=0, concat_axis=0, tiled=True)


def plan(doc_lengths, stored_block_order):
    cell = lax.axis_index("ctx")
    starts = jnp.cumsum(doc_lengths) - doc_lengths
    window_first = (cell - (SLOTS - 1)) * CELL_BLOCKS
    padded = jnp.pad(stored_block_order, (WINDOW_BLOCKS - CELL_BLOCKS, 0))
    window_order = lax.dynamic_slice_in_dim(padded, cell * CELL_BLOCKS, WINDOW_BLOCKS, 0)
    base = jnp.arange(WINDOW_BLOCKS, dtype=jnp.int32) // CELL_BLOCKS * CELL_BLOCKS
    place = base + window_order % CELL_BLOCKS
    own_place = place[WINDOW_BLOCKS - CELL_BLOCKS :]
    own_block = window_first + own_place
    token = lax.broadcasted_iota(jnp.int32, (CELL_BLOCKS, 1, ROWS), 2) // SHARE
    pos = own_block[:, None, None] * BLOCK + token
    begun = starts <= pos[..., None]
    doc_start = jnp.max(jnp.where(begun, starts, 0), axis=-1)
    doc_rows = (doc_start - window_first * BLOCK).astype(jnp.int32)
    edges = jnp.concatenate([own_block * BLOCK, own_block * BLOCK + BLOCK - 1])
    low = jnp.max(jnp.where(starts <= edges[:, None], starts, 0), axis=-1) - window_first * BLOCK
    scal = jnp.concatenate([place, own_place, low[:CELL_BLOCKS] // BLOCK, low[CELL_BLOCKS:]]).astype(jnp.int32)
    return scal, doc_rows


def body(queries, keys, values, out_grad, doc_lengths, stored_block_order):
    scal, doc_rows = plan(doc_lengths, stored_block_order)
    first_in = exchanged(jnp.concatenate([by_head(queries), by_head(keys), by_head(values)], axis=1))
    kv0 = first_in[:, HALF:, :]
    kv = (kv0, passed_along(kv0, "ctx", 1), passed_along(kv0, "ctx", 2))
    grad_in = exchanged(by_head(out_grad))
    rows_out, dkv0, dkv1, dkv2 = attention(scal, first_in, grad_in, doc_rows, kv)
    near, far = passed_along(dkv1, "ctx", -1), passed_along(dkv2, "ctx", -2)
    rows_in = exchanged(rows_out)
    summed = dkv0.astype(jnp.float32) + near.astype(jnp.float32) + far.astype(jnp.float32)
    summed, rows_in = lax.optimization_barrier((summed.astype(jnp.bfloat16), rows_in))
    sums_in = exchanged(summed)
    tokens = queries.shape[0]

    def by_token(block, heads):
        return block.reshape(8, tokens, heads, HEAD_SIZE).transpose(1, 0, 2, 3).reshape(tokens, -1, HEAD_SIZE)

    attended, query_grad = by_token(rows_in[:, :HALF], SHARE), by_token(rows_in[:, HALF:], SHARE)
    key_gradient, value_gradient = by_token(sums_in[:, :64], 1), by_token(sums_in[:, 64:], 1)
    return attended, query_grad, key_gradient, value_gradient


def solution(mesh):
    spec = P(("ctx", "head"), None, None)
    return jax.shard_map(
        body,
        mesh=mesh,
        in_specs=(spec, spec, spec, spec, P(), P()),
        out_specs=(spec, spec, spec, spec),
        check_vma=False,
    )
```

```python
import functools
import math

import jax
import jax.numpy as jnp
from jax import lax
from jax.experimental import pallas as pl
from jax.experimental.pallas import tpu as pltpu
from jax.sharding import PartitionSpec as P

HEAD_SIZE = 128
BLOCK = 128
CELL_BLOCKS = 4
SLOTS = 3
WINDOW_BLOCKS = SLOTS * CELL_BLOCKS
WINDOW = WINDOW_BLOCKS * BLOCK
CHUNK = 2 * BLOCK
PADDED = WINDOW + BLOCK
REACH = 10 * BLOCK
SHARE = 8
HALF = 64 * SHARE
ROWS = 2 * HALF

SCALE = HEAD_SIZE ** (-0.5)
EXP2_SCALE = SCALE * math.log2(math.e)
NEG_BIG = -1e30

NT = (((1,), (1,)), ((), ()))
NN = (((1,), (0,)), ((), ()))
TN = (((0,), (0,)), ((), ()))


def dot(a, b, dims=NN):
    return lax.dot_general(a, b, dims, preferred_element_type=jnp.float32)


def passed_along(block, axis, distance):
    devices = range(lax.axis_size(axis))
    route = [(i - distance, i) for i in devices if i - distance in devices]
    return lax.ppermute(block, axis, route)


def stored_rows(kv_ref, block, which):
    first = kv_ref[2 * block, pl.ds(64 * which, 64), :]
    second = kv_ref[2 * block + 1, pl.ds(64 * which, 64), :]
    return jnp.concatenate([first, second], axis=0)


def window_start(scal_ref, slot, block):
    index = (SLOTS - 1 - slot) * CELL_BLOCKS + block
    return pl.multiple_of(scal_ref[index] * BLOCK, BLOCK)


def allowed_tile(key_start, count, first_block, doc_start, tile):
    lane = lax.broadcasted_iota(jnp.int32, (1, HALF), 1) + tile * HALF
    query_pos = first_block * BLOCK + lax.shift_right_logical(lane, 3)
    key_pos = lax.broadcasted_iota(jnp.int32, (count, HALF), 0)
    return (key_pos >= doc_start - key_start) & (key_pos <= query_pos - key_start)


def attention_kernel(scal_ref, q_ref, grad_ref, doc_ref, kv0_ref, kv1_ref, kv2_ref, att_ref, dq_ref, dkv0_ref, dkv1_ref, dkv2_ref, key_seq, value_seq, value_t, scores, acc, top, dq_acc, dk_acc, dv_acc, weights_low, grads_low):
    step = pl.program_id(0)

    @pl.when(step == 0)
    def _():
        for slot, kv_ref in enumerate((kv0_ref, kv1_ref, kv2_ref)):
            for block in range(CELL_BLOCKS):
                start = window_start(scal_ref, slot, block)
                key_seq[pl.ds(start, BLOCK), :] = stored_rows(kv_ref, block, 0)
                value = stored_rows(kv_ref, block, 1)
                value_seq[pl.ds(start, BLOCK), :] = value
                value_t[:, pl.ds(start, BLOCK)] = value.astype(jnp.float32).T.astype(jnp.bfloat16)
        zeros = jnp.zeros((BLOCK, HEAD_SIZE), jnp.bfloat16)
        key_seq[pl.ds(WINDOW, BLOCK), :] = zeros
        value_seq[pl.ds(WINDOW, BLOCK), :] = zeros
        value_t[:, pl.ds(WINDOW, BLOCK)] = zeros
        dk_acc[...] = jnp.zeros_like(dk_acc)
        dv_acc[...] = jnp.zeros_like(dv_acc)

    first_block = scal_ref[WINDOW_BLOCKS + step]
    low_block = scal_ref[WINDOW_BLOCKS + CELL_BLOCKS + step]
    last_start = scal_ref[WINDOW_BLOCKS + 2 * CELL_BLOCKS + step]
    chunks = lax.shift_right_logical(first_block - low_block + 2, 1)
    pairs = lax.shift_right_logical(chunks, 1)
    top[...] = jnp.full_like(top, NEG_BIG)
    acc[...] = jnp.zeros_like(acc)
    dq_acc[...] = jnp.zeros_like(dq_acc)

    def span(turn, count):
        key_start = pl.multiple_of((low_block + 4 * turn) * BLOCK, BLOCK)
        return key_start, pl.ds(key_start, count), pl.ds(pl.multiple_of(turn * 2 * CHUNK, CHUNK), count)

    def score(turn, count, masked):
        key_start, window, rows = span(turn, count)
        for tile in range(2):
            cols = slice(tile * HALF, (tile + 1) * HALF)
            raw = dot(key_seq[window, :], q_ref[tile], NT)
            if masked:
                allowed = allowed_tile(key_start, count, first_block, doc_ref[0, :, cols], tile)
                raw = jnp.where(allowed, raw, NEG_BIG)
            scores[rows, cols] = raw
            top[:, cols] = jnp.maximum(top[:, cols], jnp.max(raw.reshape(count // 8, 8, HALF), axis=0))

    def score_pair(turn, _):
        key_start = (low_block + 4 * turn) * BLOCK
        whole = (key_start >= last_start) & (key_start + 2 * CHUNK <= first_block * BLOCK)
        pl.when(whole)(lambda: score(turn, 2 * CHUNK, False))
        pl.when(jnp.logical_not(whole))(lambda: score(turn, 2 * CHUNK, True))
        return 0

    lax.fori_loop(0, pairs, score_pair, 0)
    pl.when(chunks > 2 * pairs)(lambda: score(pairs, CHUNK, True))
    highest = jnp.max(top[...], axis=0, keepdims=True) * EXP2_SCALE
    top[...] = jnp.zeros_like(top)

    def weigh(turn, count):
        _, window, rows = span(turn, count)
        for tile in range(2):
            cols = slice(tile * HALF, (tile + 1) * HALF)
            weights = jnp.exp2(scores[rows, cols] * EXP2_SCALE - highest[:, cols])
            top[:, cols] += jnp.sum(weights.reshape(count // 8, 8, HALF), axis=0)
            acc[:, cols] += dot(value_t[:, window], weights.astype(jnp.bfloat16))

    def weigh_pair(turn, _):
        weigh(turn, 2 * CHUNK)
        return 0

    lax.fori_loop(0, pairs, weigh_pair, 0)
    pl.when(chunks > 2 * pairs)(lambda: weigh(pairs, CHUNK))
    total = jnp.sum(top[...], axis=0, keepdims=True)
    lse = highest + jnp.log2(total)
    out = (acc[...] * (1.0 / total)).T.astype(jnp.bfloat16)
    att_ref[...] = out.reshape(2, HALF, HEAD_SIZE)
    delta = jnp.sum((out.astype(jnp.float32) * grad_ref[...].reshape(ROWS, HEAD_SIZE).astype(jnp.float32)).T, axis=0, keepdims=True)

    def grad_chunk(turn, _):
        window = pl.ds(pl.multiple_of((low_block + 2 * turn) * BLOCK, BLOCK), CHUNK)
        rows = pl.ds(pl.multiple_of(turn * CHUNK, CHUNK), CHUNK)
        keys = key_seq[window, :]
        for tile in range(2):
            cols = slice(tile * HALF, (tile + 1) * HALF)
            weights = jnp.exp2(scores[rows, cols] * EXP2_SCALE - lse[:, cols])
            weights_low[:, cols] = weights.astype(jnp.bfloat16)
            sent = dot(value_seq[window, :], grad_ref[tile], NT)
            grads_low[:, cols] = (weights * (sent - delta[:, cols])).astype(jnp.bfloat16)
        dq_acc[...] += dot(grads_low[...], keys, TN)
        dk_acc[window, :] += dot(grads_low[...], q_ref[...].reshape(ROWS, HEAD_SIZE))
        dv_acc[window, :] += dot(weights_low[...], grad_ref[...].reshape(ROWS, HEAD_SIZE))
        return 0

    lax.fori_loop(0, chunks, grad_chunk, 0)
    query_grad = (dq_acc[...] * SCALE).astype(jnp.bfloat16)
    dq_ref[...] = query_grad.reshape(2, HALF, HEAD_SIZE)

    @pl.when(step == CELL_BLOCKS - 1)
    def _():
        for slot, dkv_ref in enumerate((dkv0_ref, dkv1_ref, dkv2_ref)):
            for block in range(CELL_BLOCKS):
                start = window_start(scal_ref, slot, block)
                dk = (dk_acc[pl.ds(start, BLOCK), :] * SCALE).astype(jnp.bfloat16)
                dv = dv_acc[pl.ds(start, BLOCK), :].astype(jnp.bfloat16)
                for half in range(2):
                    rows = slice(half * 64, (half + 1) * 64)
                    dkv_ref[2 * block + half, pl.ds(0, 64), :] = dk[rows]
                    dkv_ref[2 * block + half, pl.ds(64, 64), :] = dv[rows]


def attention(scal, q_in, grad_in, doc_rows, kv):
    row_spec = pl.BlockSpec((2, HALF, HEAD_SIZE), lambda b, s: (b, 0, 0))
    kv_spec = pl.BlockSpec((8, 128, HEAD_SIZE), lambda b, s: (0, 0, 0))
    return pl.pallas_call(
        attention_kernel,
        grid_spec=pltpu.PrefetchScalarGridSpec(
            num_scalar_prefetch=1,
            grid=(CELL_BLOCKS,),
            in_specs=[row_spec, row_spec, pl.BlockSpec((1, 1, ROWS), lambda b, s: (b, 0, 0))] + [kv_spec] * 3,
            out_specs=[row_spec, row_spec] + [kv_spec] * 3,
            scratch_shapes=[
                pltpu.VMEM((PADDED, HEAD_SIZE), jnp.bfloat16),
                pltpu.VMEM((PADDED, HEAD_SIZE), jnp.bfloat16),
                pltpu.VMEM((HEAD_SIZE, PADDED), jnp.bfloat16),
                pltpu.VMEM((REACH, ROWS), jnp.float32),
                pltpu.VMEM((HEAD_SIZE, ROWS), jnp.float32),
                pltpu.VMEM((8, ROWS), jnp.float32),
                pltpu.VMEM((ROWS, HEAD_SIZE), jnp.float32),
                pltpu.VMEM((PADDED, HEAD_SIZE), jnp.float32),
                pltpu.VMEM((PADDED, HEAD_SIZE), jnp.float32),
                pltpu.VMEM((CHUNK, ROWS), jnp.bfloat16),
                pltpu.VMEM((CHUNK, ROWS), jnp.bfloat16),
            ],
        ),
        out_shape=[jax.ShapeDtypeStruct((8, rows, HEAD_SIZE), jnp.bfloat16) for rows in (HALF, HALF + 128)] + [jax.ShapeDtypeStruct((8, 128, HEAD_SIZE), jnp.bfloat16)] * 3,
        compiler_params=pltpu.CompilerParams(dimension_semantics=("arbitrary",), vmem_limit_bytes=60 * 1024 * 1024),
        cost_estimate=pl.CostEstimate(flops=10_000_000_000, bytes_accessed=6_000_000, transcendentals=4_000_000),
        name="attention",
    )(scal, q_in, grad_in, doc_rows, *kv)


def by_head(rows):
    tokens = rows.shape[0]
    split = rows.reshape(tokens, 8, -1, HEAD_SIZE).transpose(1, 0, 2, 3)
    return split.reshape(8, -1, HEAD_SIZE)


def exchanged(block):
    return lax.all_to_all(block, "head", split_axis=0, concat_axis=0, tiled=True)


def plan(doc_lengths, stored_block_order):
    cell = lax.axis_index("ctx")
    starts = jnp.cumsum(doc_lengths) - doc_lengths
    window_first = (cell - (SLOTS - 1)) * CELL_BLOCKS
    padded = jnp.pad(stored_block_order, (WINDOW_BLOCKS - CELL_BLOCKS, 0))
    window_order = lax.dynamic_slice_in_dim(padded, cell * CELL_BLOCKS, WINDOW_BLOCKS, 0)
    base = jnp.arange(WINDOW_BLOCKS, dtype=jnp.int32) // CELL_BLOCKS * CELL_BLOCKS
    place = base + window_order % CELL_BLOCKS
    own_place = place[WINDOW_BLOCKS - CELL_BLOCKS :]
    own_block = window_first + own_place
    token = lax.broadcasted_iota(jnp.int32, (CELL_BLOCKS, 1, ROWS), 2) // SHARE
    pos = own_block[:, None, None] * BLOCK + token
    begun = starts <= pos[..., None]
    doc_start = jnp.max(jnp.where(begun, starts, 0), axis=-1)
    doc_rows = (doc_start - window_first * BLOCK).astype(jnp.int32)
    edges = jnp.concatenate([own_block * BLOCK, own_block * BLOCK + BLOCK - 1])
    low = jnp.max(jnp.where(starts <= edges[:, None], starts, 0), axis=-1) - window_first * BLOCK
    scal = jnp.concatenate([place, own_place, low[:CELL_BLOCKS] // BLOCK, low[CELL_BLOCKS:]]).astype(jnp.int32)
    return scal, doc_rows


def body(queries, keys, values, out_grad, doc_lengths, stored_block_order):
    scal, doc_rows = plan(doc_lengths, stored_block_order)
    first_in = exchanged(jnp.concatenate([by_head(queries), by_head(keys), by_head(values)], axis=1))
    kv0 = first_in[:, HALF:, :]
    kv = (kv0, passed_along(kv0, "ctx", 1), passed_along(kv0, "ctx", 2))
    grad_in = exchanged(by_head(out_grad))
    attended_loc, last_loc, dkv0, dkv1, dkv2 = attention(scal, first_in, grad_in, doc_rows, kv)
    near, far = passed_along(dkv1, "ctx", -1), passed_along(dkv2, "ctx", -2)
    attended_in = exchanged(attended_loc)
    summed = dkv0.astype(jnp.float32) + near.astype(jnp.float32) + far.astype(jnp.float32)
    last_loc = lax.dynamic_update_slice(last_loc, summed.astype(jnp.bfloat16), (0, HALF, 0))
    last_loc, attended_in = lax.optimization_barrier((last_loc, attended_in))
    last_in = exchanged(last_loc)
    tokens = queries.shape[0]

    def by_token(block, heads):
        return block.reshape(8, tokens, heads, HEAD_SIZE).transpose(1, 0, 2, 3).reshape(tokens, -1, HEAD_SIZE)

    attended, query_grad = by_token(attended_in, SHARE), by_token(last_in[:, :HALF], SHARE)
    key_gradient = by_token(last_in[:, HALF : HALF + 64], 1)
    value_gradient = by_token(last_in[:, HALF + 64 :], 1)
    return attended, query_grad, key_gradient, value_gradient


def solution(mesh):
    spec = P(("ctx", "head"), None, None)
    return jax.shard_map(
        body,
        mesh=mesh,
        in_specs=(spec, spec, spec, spec, P(), P()),
        out_specs=(spec, spec, spec, spec),
        check_vma=False,
    )
```

```python
import functools
import math

import jax
import jax.numpy as jnp
from jax import lax
from jax.experimental import pallas as pl
from jax.experimental.pallas import tpu as pltpu
from jax.sharding import PartitionSpec as P

HEAD_SIZE = 128
BLOCK = 128
CELL_BLOCKS = 4
SLOTS = 3
WINDOW_BLOCKS = SLOTS * CELL_BLOCKS
WINDOW = WINDOW_BLOCKS * BLOCK
CHUNK = 2 * BLOCK
PADDED = WINDOW + BLOCK
REACH = 10 * BLOCK
SHARE = 8
ROWS = BLOCK * SHARE
TILE = ROWS // 2

SCALE = HEAD_SIZE ** (-0.5)
EXP2_SCALE = SCALE * math.log2(math.e)
NEG_BIG = -1e30

NT = (((1,), (1,)), ((), ()))
NN = (((1,), (0,)), ((), ()))
TN = (((0,), (0,)), ((), ()))


def dot(a, b, dims=NN):
    return lax.dot_general(a, b, dims, preferred_element_type=jnp.float32)


def passed_along(block, axis, distance):
    devices = range(lax.axis_size(axis))
    route = [(i - distance, i) for i in devices if i - distance in devices]
    return lax.ppermute(block, axis, route)


def stored_rows(kv_ref, block, which):
    first = kv_ref[2 * block, pl.ds(64 * which, 64), :]
    second = kv_ref[2 * block + 1, pl.ds(64 * which, 64), :]
    return jnp.concatenate([first, second], axis=0)


def window_start(scal_ref, slot, block):
    index = (SLOTS - 1 - slot) * CELL_BLOCKS + block
    return pl.multiple_of(scal_ref[index] * BLOCK, BLOCK)


def allowed_tile(key_start, first_block, doc_start, tile, count=CHUNK):
    lane = lax.broadcasted_iota(jnp.int32, (1, TILE), 1) + tile * TILE
    query_pos = first_block * BLOCK + lax.shift_right_logical(lane, 3)
    key_pos = lax.broadcasted_iota(jnp.int32, (count, TILE), 0)
    return (key_pos >= doc_start - key_start) & (key_pos <= query_pos - key_start)


def each_chunk(scal_ref, step, work):
    first_block = scal_ref[WINDOW_BLOCKS + step]
    low_block = scal_ref[WINDOW_BLOCKS + CELL_BLOCKS + step]
    last_start = scal_ref[WINDOW_BLOCKS + 2 * CELL_BLOCKS + step]
    chunks = lax.shift_right_logical(first_block - low_block + 2, 1)

    def turn_work(turn, _):
        key_start = pl.multiple_of((low_block + 2 * turn) * BLOCK, BLOCK)
        whole = (key_start >= last_start) & (key_start + CHUNK <= first_block * BLOCK)

        @pl.when(whole)
        def _():
            work(turn, key_start, first_block, False)

        @pl.when(jnp.logical_not(whole))
        def _():
            work(turn, key_start, first_block, True)

        return 0

    lax.fori_loop(0, chunks, turn_work, 0)


def forward_kernel(scal_ref, q_ref, doc_ref, kv0_ref, kv1_ref, kv2_ref, out_ref, out_t_ref, lse_ref, key_seq, value_t, scores, acc, top):
    step = pl.program_id(0)

    @pl.when(step == 0)
    def _():
        for slot, kv_ref in enumerate((kv0_ref, kv1_ref, kv2_ref)):
            for block in range(CELL_BLOCKS):
                start = window_start(scal_ref, slot, block)
                key_seq[pl.ds(start, BLOCK), :] = stored_rows(kv_ref, block, 0)
                value = stored_rows(kv_ref, block, 1).astype(jnp.float32)
                value_t[:, pl.ds(start, BLOCK)] = value.T.astype(jnp.bfloat16)
        key_seq[pl.ds(WINDOW, BLOCK), :] = jnp.zeros((BLOCK, HEAD_SIZE), jnp.bfloat16)
        value_t[:, pl.ds(WINDOW, BLOCK)] = jnp.zeros((HEAD_SIZE, BLOCK), jnp.bfloat16)

    top[...] = jnp.full_like(top, NEG_BIG)
    acc[...] = jnp.zeros_like(acc)

    first_block = scal_ref[WINDOW_BLOCKS + step]
    low_block = scal_ref[WINDOW_BLOCKS + CELL_BLOCKS + step]
    last_start = scal_ref[WINDOW_BLOCKS + 2 * CELL_BLOCKS + step]
    chunks = lax.shift_right_logical(first_block - low_block + 2, 1)
    pairs = lax.shift_right_logical(chunks, 1)

    def score(turn, count, masked):
        key_start = pl.multiple_of((low_block + 4 * turn) * BLOCK, BLOCK)
        keys = key_seq[pl.ds(key_start, count), :]
        rows = pl.ds(pl.multiple_of(turn * 2 * CHUNK, CHUNK), count)
        for tile in range(2):
            cols = slice(tile * TILE, (tile + 1) * TILE)
            raw = dot(keys, q_ref[tile], NT)
            if masked:
                allowed = allowed_tile(key_start, first_block, doc_ref[0, :, cols], tile, count)
                raw = jnp.where(allowed, raw, NEG_BIG)
            scores[rows, cols] = raw
            part = jnp.max(raw.reshape(count // 8, 8, TILE), axis=0)
            top[:, cols] = jnp.maximum(top[:, cols], part)

    def score_pair(turn, _):
        key_start = (low_block + 4 * turn) * BLOCK
        whole = (key_start >= last_start) & (key_start + 2 * CHUNK <= first_block * BLOCK)
        pl.when(whole)(lambda: score(turn, 2 * CHUNK, False))
        pl.when(jnp.logical_not(whole))(lambda: score(turn, 2 * CHUNK, True))
        return 0

    lax.fori_loop(0, pairs, score_pair, 0)
    pl.when(chunks > 2 * pairs)(lambda: score(pairs, CHUNK, True))
    highest = jnp.max(top[...], axis=0, keepdims=True) * EXP2_SCALE
    top[...] = jnp.zeros_like(top)

    def weigh(turn, count):
        key_start = pl.multiple_of((low_block + 4 * turn) * BLOCK, BLOCK)
        rows = pl.ds(pl.multiple_of(turn * 2 * CHUNK, CHUNK), count)
        values = value_t[:, pl.ds(key_start, count)]
        for tile in range(2):
            cols = slice(tile * TILE, (tile + 1) * TILE)
            weights = jnp.exp2(scores[rows, cols] * EXP2_SCALE - highest[:, cols])
            top[:, cols] += jnp.sum(weights.reshape(count // 8, 8, TILE), axis=0)
            acc[:, cols] += dot(values, weights.astype(jnp.bfloat16))

    def weigh_pair(turn, _):
        weigh(turn, 2 * CHUNK)
        return 0

    lax.fori_loop(0, pairs, weigh_pair, 0)
    pl.when(chunks > 2 * pairs)(lambda: weigh(pairs, CHUNK))
    total = jnp.sum(top[...], axis=0, keepdims=True)
    lse_ref[0] = highest + jnp.log2(total)
    out_t = acc[...] * (1.0 / total)
    out_t_ref[0] = out_t.astype(jnp.bfloat16)
    out = out_t.T.astype(jnp.bfloat16)
    out_ref[0] = out[: ROWS // 2]
    out_ref[1] = out[ROWS // 2 :]


def backward_kernel(scal_ref, q_ref, grad_ref, out_t_ref, lse_ref, doc_ref, kv0_ref, kv1_ref, kv2_ref, dq_ref, dkv0_ref, dkv1_ref, dkv2_ref, key_seq, value_seq, dk_acc, dv_acc, dq_acc, weights_low, grads_low, delta):
    step = pl.program_id(0)

    @pl.when(step == 0)
    def _():
        for slot, kv_ref in enumerate((kv0_ref, kv1_ref, kv2_ref)):
            for block in range(CELL_BLOCKS):
                start = window_start(scal_ref, slot, block)
                key_seq[pl.ds(start, BLOCK), :] = stored_rows(kv_ref, block, 0)
                value_seq[pl.ds(start, BLOCK), :] = stored_rows(kv_ref, block, 1)
        zeros = jnp.zeros((BLOCK, HEAD_SIZE), jnp.bfloat16)
        key_seq[pl.ds(WINDOW, BLOCK), :] = zeros
        value_seq[pl.ds(WINDOW, BLOCK), :] = zeros
        dk_acc[...] = jnp.zeros_like(dk_acc)
        dv_acc[...] = jnp.zeros_like(dv_acc)

    dq_acc[...] = jnp.zeros_like(dq_acc)
    for half in range(2):
        cols = slice(half * TILE, (half + 1) * TILE)
        grad_t = grad_ref[half].astype(jnp.float32).T
        delta[:, cols] = jnp.sum(grad_t * out_t_ref[0, :, cols].astype(jnp.float32), axis=0, keepdims=True)

    def chunk(turn, key_start, first_block, masked):
        keys = key_seq[pl.ds(key_start, CHUNK), :]
        values = value_seq[pl.ds(key_start, CHUNK), :]
        for tile in range(2):
            cols = slice(tile * TILE, (tile + 1) * TILE)
            raw = dot(keys, q_ref[tile], NT)
            scaled = raw * EXP2_SCALE - lse_ref[0, :, cols]
            if masked:
                scaled = jnp.where(allowed_tile(key_start, first_block, doc_ref[0, :, cols], tile), scaled, NEG_BIG)
            weights = jnp.exp2(scaled)
            weights_low[:, cols] = weights.astype(jnp.bfloat16)
            sent = dot(values, grad_ref[tile], NT)
            grads_low[:, cols] = (weights * (sent - delta[:, cols])).astype(jnp.bfloat16)
        queries = jnp.concatenate([q_ref[0], q_ref[1]], axis=0)
        out_grads = jnp.concatenate([grad_ref[0], grad_ref[1]], axis=0)
        dq_acc[...] += dot(grads_low[...], keys, TN)
        dk_acc[pl.ds(key_start, CHUNK), :] += dot(grads_low[...], queries)
        dv_acc[pl.ds(key_start, CHUNK), :] += dot(weights_low[...], out_grads)

    each_chunk(scal_ref, step, chunk)
    query_grad = (dq_acc[...] * SCALE).astype(jnp.bfloat16)
    dq_ref[0] = query_grad[:TILE]
    dq_ref[1] = query_grad[TILE:]

    @pl.when(step == CELL_BLOCKS - 1)
    def _():
        for slot, dkv_ref in enumerate((dkv0_ref, dkv1_ref, dkv2_ref)):
            for block in range(CELL_BLOCKS):
                start = window_start(scal_ref, slot, block)
                dk = (dk_acc[pl.ds(start, BLOCK), :] * SCALE).astype(jnp.bfloat16)
                dv = dv_acc[pl.ds(start, BLOCK), :].astype(jnp.bfloat16)
                for half in range(2):
                    rows = slice(half * 64, (half + 1) * 64)
                    dkv_ref[2 * block + half, pl.ds(0, 64), :] = dk[rows]
                    dkv_ref[2 * block + half, pl.ds(64, 64), :] = dv[rows]


def row_spec():
    return pl.BlockSpec((2, ROWS // 2, HEAD_SIZE), lambda b, s: (b, 0, 0))


def lane_spec(rows):
    return pl.BlockSpec((1, rows, ROWS), lambda b, s: (b, 0, 0))


def kv_spec():
    return pl.BlockSpec((8, 128, HEAD_SIZE), lambda b, s: (0, 0, 0))


def params(mebibytes):
    return pltpu.CompilerParams(dimension_semantics=("arbitrary",), vmem_limit_bytes=mebibytes * 1024 * 1024)


def forward(scal, q_in, doc_rows, kv):
    return pl.pallas_call(
        forward_kernel,
        grid_spec=pltpu.PrefetchScalarGridSpec(
            num_scalar_prefetch=1,
            grid=(CELL_BLOCKS,),
            in_specs=[row_spec(), lane_spec(1), kv_spec(), kv_spec(), kv_spec()],
            out_specs=[row_spec(), lane_spec(HEAD_SIZE), lane_spec(1)],
            scratch_shapes=[
                pltpu.VMEM((PADDED, HEAD_SIZE), jnp.bfloat16),
                pltpu.VMEM((HEAD_SIZE, PADDED), jnp.bfloat16),
                pltpu.VMEM((REACH, ROWS), jnp.float32),
                pltpu.VMEM((HEAD_SIZE, ROWS), jnp.float32),
                pltpu.VMEM((8, ROWS), jnp.float32),
            ],
        ),
        out_shape=[
            jax.ShapeDtypeStruct((8, ROWS // 2, HEAD_SIZE), jnp.bfloat16),
            jax.ShapeDtypeStruct((CELL_BLOCKS, HEAD_SIZE, ROWS), jnp.bfloat16),
            jax.ShapeDtypeStruct((CELL_BLOCKS, 1, ROWS), jnp.float32),
        ],
        compiler_params=params(60),
        cost_estimate=pl.CostEstimate(flops=4_000_000_000, bytes_accessed=4_000_000, transcendentals=4_000_000),
        name="forward",
    )(scal, q_in, doc_rows, *kv)


def backward(scal, q_in, grad_in, out_t, lse, doc_rows, kv):
    dkv_shape = jax.ShapeDtypeStruct((8, 128, HEAD_SIZE), jnp.bfloat16)
    return pl.pallas_call(
        backward_kernel,
        grid_spec=pltpu.PrefetchScalarGridSpec(
            num_scalar_prefetch=1,
            grid=(CELL_BLOCKS,),
            in_specs=[row_spec(), row_spec(), lane_spec(HEAD_SIZE), lane_spec(1), lane_spec(1), kv_spec(), kv_spec(), kv_spec()],
            out_specs=[row_spec(), kv_spec(), kv_spec(), kv_spec()],
            scratch_shapes=[
                pltpu.VMEM((PADDED, HEAD_SIZE), jnp.bfloat16),
                pltpu.VMEM((PADDED, HEAD_SIZE), jnp.bfloat16),
                pltpu.VMEM((PADDED, HEAD_SIZE), jnp.float32),
                pltpu.VMEM((PADDED, HEAD_SIZE), jnp.float32),
                pltpu.VMEM((ROWS, HEAD_SIZE), jnp.float32),
                pltpu.VMEM((CHUNK, ROWS), jnp.bfloat16),
                pltpu.VMEM((CHUNK, ROWS), jnp.bfloat16),
                pltpu.VMEM((1, ROWS), jnp.float32),
            ],
        ),
        out_shape=[jax.ShapeDtypeStruct((8, ROWS // 2 + 128, HEAD_SIZE), jnp.bfloat16), dkv_shape, dkv_shape, dkv_shape],
        compiler_params=params(59),
        cost_estimate=pl.CostEstimate(flops=10_000_000_000, bytes_accessed=6_000_000, transcendentals=4_000_000),
        name="backward",
    )(scal, q_in, grad_in, out_t, lse, doc_rows, *kv)


def by_head(rows):
    tokens = rows.shape[0]
    split = rows.reshape(tokens, 8, -1, HEAD_SIZE).transpose(1, 0, 2, 3)
    return split.reshape(8, -1, HEAD_SIZE)


def exchanged(block):
    return lax.all_to_all(block, "head", split_axis=0, concat_axis=0, tiled=True)


def plan(doc_lengths, stored_block_order):
    cell = lax.axis_index("ctx")
    starts = jnp.cumsum(doc_lengths) - doc_lengths
    window_first = (cell - (SLOTS - 1)) * CELL_BLOCKS
    padded = jnp.pad(stored_block_order, (WINDOW_BLOCKS - CELL_BLOCKS, 0))
    window_order = lax.dynamic_slice_in_dim(padded, cell * CELL_BLOCKS, WINDOW_BLOCKS, 0)
    base = jnp.arange(WINDOW_BLOCKS, dtype=jnp.int32) // CELL_BLOCKS * CELL_BLOCKS
    place = base + window_order % CELL_BLOCKS
    own_place = place[WINDOW_BLOCKS - CELL_BLOCKS :]
    own_block = window_first + own_place
    token = lax.broadcasted_iota(jnp.int32, (CELL_BLOCKS, 1, ROWS), 2) // SHARE
    pos = own_block[:, None, None] * BLOCK + token
    begun = starts <= pos[..., None]
    doc_start = jnp.max(jnp.where(begun, starts, 0), axis=-1)
    doc_rows = doc_start - window_first * BLOCK
    edges = jnp.concatenate([own_block * BLOCK, own_block * BLOCK + BLOCK - 1])
    low = jnp.max(jnp.where(starts <= edges[:, None], starts, 0), axis=-1) - window_first * BLOCK
    scal = jnp.concatenate([place, own_place, low[:CELL_BLOCKS] // BLOCK, low[CELL_BLOCKS:]]).astype(jnp.int32)
    return scal, doc_rows.astype(jnp.int32)


def body(queries, keys, values, out_grad, doc_lengths, stored_block_order):
    scal, doc_rows = plan(doc_lengths, stored_block_order)
    first_in = exchanged(jnp.concatenate([by_head(queries), by_head(keys), by_head(values)], axis=1))
    kv0 = first_in[:, 512:, :]
    kv = (kv0, passed_along(kv0, "ctx", 1), passed_along(kv0, "ctx", 2))
    grad_rows, *kv = lax.optimization_barrier((by_head(out_grad), *kv))
    grad_in = exchanged(grad_rows)
    attended_loc, out_t, lse = forward(scal, first_in, doc_rows, kv)
    attended_in = exchanged(attended_loc)
    last_loc, dkv0, dkv1, dkv2 = backward(scal, first_in, grad_in, out_t, lse, doc_rows, kv)
    attended_in, dkv1, dkv2 = lax.optimization_barrier((attended_in, dkv1, dkv2))
    near, far = passed_along(dkv1, "ctx", -1), passed_along(dkv2, "ctx", -2)
    summed = dkv0.astype(jnp.float32) + near.astype(jnp.float32) + far.astype(jnp.float32)
    last_loc = lax.dynamic_update_slice(last_loc, summed.astype(jnp.bfloat16), (0, 512, 0))
    last_in = exchanged(last_loc)
    tokens = queries.shape[0]

    def by_token(block, heads):
        return block.reshape(8, tokens, heads, HEAD_SIZE).transpose(1, 0, 2, 3).reshape(tokens, -1, HEAD_SIZE)

    attended = by_token(attended_in, SHARE)
    query_grad = by_token(last_in[:, :512], SHARE)
    key_gradient = by_token(last_in[:, 512:576], 1)
    value_gradient = by_token(last_in[:, 576:], 1)
    return attended, query_grad, key_gradient, value_gradient


def solution(mesh):
    spec = P(("ctx", "head"), None, None)
    return jax.shard_map(
        body,
        mesh=mesh,
        in_specs=(spec, spec, spec, spec, P(), P()),
        out_specs=(spec, spec, spec, spec),
        check_vma=False,
    )
```
